32 devices in a mesh: groups: 2 (over y), area: 8 (over z, x), row: 2 (over core).
Axes of the slice: x: 2, y: 2, z: 4, core: 2. Of those that a mesh axis runs over, the one named last changes fastest.
Arguments:
- proj_index: int32 [8, 384], P('area', 'row'), may hold values from 0 to 2047
- delays: int32 [8, 2], P('area'), may hold values from 3 to 5
- past_rates: bfloat16 [8, 6, 128, 384], P('area', None, 'groups', 'row'), parts along dimension 2, may hold values from -0.8984375 to 0.8984375
- potential: float32 [8, 128, 4096], P('area', 'groups', 'row'), parts along dimension 1, may hold values from -6 to 6
- stimulus: float32 [8, 128, 4096], P('area', 'groups', 'row'), parts along dimension 1, may hold values from -5 to 5
- leak_rate: float32 [8, 4096], P('area', 'row'), may hold values from 0.1 to 0.6
- recurrence: bfloat16 [8, 4096, 4096], P('area', None, 'row'), may hold values from -0.09375 to 0.09375
- ff_weight: bfloat16 [8, 192, 4096], P('area', None, 'row'), may hold values from -0.4375 to 0.4375
- fb_weight: bfloat16 [8, 192, 4096], P('area', None, 'row'), may hold values from -0.4375 to 0.4375
Outputs:
- final_potential: float32 [8, 128, 4096], P('area', 'groups', 'row'), parts along dimension 1
The draws below stay inside these ranges and needn't reach their ends.
There are 2 independent parts, one for each index of `groups`. The reference program is written for one: setup_inputs(seed, part) draws one part's arguments, and reference() takes and returns one part's arrays. A program takes and returns all parts, laid end to end along the dimension named above; an argument that names none is the same for every part. Nothing has to cross between parts.
Inputs may be any that keep to these rules, and one draw needn't show every extreme that they name: `proj_index`: indices within a block of 2048 neurons.
All inputs are finite; a program needn't handle non-finite values.
Results may differ from the reference program's by a relative error of at most 0.0013.
Values may be sent and summed in bfloat16 or wider, within the bound.
No kernel may reach another device: no remote copies, remote signals or barrier semaphores. Data moves between devices by JAX's collectives and lax.ppermute only.
A program may use at most 64 MiB of HBM per device.

```python
import math
import jax
import jax.numpy as jnp
from jax import lax

NEU = 4096
PROJ = 192
TR = 64
SUB = 3
OUTER = 2
AREAS = 8
PROJS = 384
N_ROW = 2


def with_ends(values, stream_key, smallest, largest):
    extent = values.shape
    spot = [jax.random.randint(jax.random.fold_in(stream_key, axis), (), 0, extent[axis]) for axis in range(len(extent))]
    values = values.at[tuple(spot)].set(smallest)
    longest = extent.index(max(extent))
    spot[longest] = (spot[longest] + 1) % extent[longest]
    return values.at[tuple(spot)].set(largest)


def levels(stream_key, extent, shards, least, high):
    factor_of, own = 1.0, jax.random.fold_in(stream_key, 6)
    for dim, shards_of in shards:
        draws = jnp.exp(jax.random.uniform(jax.random.fold_in(own, dim), (shards_of,), jnp.float32, least / len(shards), high / len(shards)))
        factor_of = factor_of * jnp.repeat(draws, extent[dim] // shards_of).reshape([-1 if axis == dim else 1 for axis in range(len(extent))])
    return factor_of


def centred(stream_key, extent, deviation, reach, shards=(), kind=jnp.bfloat16):
    factor_of = levels(stream_key, extent, shards, -0.22, 0.18) if shards else 1.0
    array = jax.random.normal(stream_key, extent, jnp.float32) * deviation * factor_of
    return jnp.minimum(jnp.maximum(array, -reach), reach).astype(kind)


def setup_inputs(seed: int = 0, part: int = 0) -> dict:
    streams_of = jax.random.split(jax.random.key(seed), 10)
    part_splits = jax.random.split(jax.random.fold_in(streams_of[9], part), 10)
    proj_index = with_ends(jax.random.randint(streams_of[0], (AREAS, PROJS), 0, NEU // N_ROW), jax.random.fold_in(streams_of[0], 1), 0, (NEU // N_ROW) - 1).astype(jnp.int32)
    delays = with_ends(jax.random.randint(streams_of[1], (AREAS, 2), SUB, 2 * SUB), jax.random.fold_in(streams_of[1], 1), SUB, (2 * SUB) - 1).astype(jnp.int32)
    past_rates = jnp.clip(jax.random.uniform(part_splits[2], (AREAS, 2 * SUB, TR, PROJS), jnp.float32, -0.8984375, 0.8984375) * levels(part_splits[2], (AREAS, 2 * SUB, TR, PROJS), ((0, 8), (3, 2)), -0.4, 0.0), -0.8984375, 0.8984375).astype(jnp.bfloat16)
    potential = centred(part_splits[3], (AREAS, TR, NEU), 1.0, 6.0, ((0, 8), (2, 2)), jnp.float32)
    stimulus = centred(part_splits[4], (AREAS, TR, NEU), 0.7, 5.0, ((0, 8), (2, 2)), jnp.float32)
    leak_rate = jnp.clip(jnp.exp(math.log(0.6) - 1.7917595 * jax.random.uniform(streams_of[5], (AREAS, NEU), jnp.float32) ** levels(streams_of[5], (AREAS, NEU), ((0, 8), (1, 2)), -0.2, 0.2)), 0.1, 0.6)
    recurrence = centred(streams_of[6], (AREAS, NEU, NEU), NEU ** -0.5, 0.09375, ((0, 8), (2, 2)))
    ff_weight = centred(streams_of[7], (AREAS, PROJ, NEU), PROJ ** -0.5, 0.4375, ((0, 8), (2, 2)))
    fb_weight = centred(streams_of[8], (AREAS, PROJ, NEU), PROJ ** -0.5, 0.4375, ((0, 8), (2, 2)))
    return dict(proj_index=proj_index, delays=delays, past_rates=past_rates, potential=potential, stimulus=stimulus, leak_rate=leak_rate, recurrence=recurrence, ff_weight=ff_weight, fb_weight=fb_weight)


def incoming(stacked, direction, lag_steps, mapping, instant):
    source = jnp.roll(stacked, direction, axis=0)
    position = (instant + 2 * SUB - lag_steps).astype(jnp.int32)
    selected_index = jnp.take_along_axis(source, position[:, None, None, None], axis=1)[:, 0]
    area_count = selected_index.shape[0]
    trials = selected_index.shape[1]
    grouped = selected_index.reshape(area_count, trials, N_ROW, PROJ).astype(jnp.float32)
    mapping_blocks = mapping.reshape(area_count, PROJ, N_ROW, NEU // N_ROW).astype(jnp.float32)
    return jnp.einsum("atrj,ajrn->atrn", grouped, mapping_blocks).reshape(area_count, trials, NEU)


def reference(proj_index, delays, past_rates, potential, stimulus, leak_rate, recurrence, ff_weight, fb_weight):
    block_rows = NEU // N_ROW
    offsets = (jnp.arange(PROJ * N_ROW, dtype=jnp.int32) // PROJ) * block_rows
    global_index = (proj_index + offsets[None, :]).astype(jnp.int32)
    area_count = potential.shape[0]
    trials = potential.shape[1]
    delay_table = jnp.broadcast_to(global_index[:, None, :], (area_count, trials, PROJ * N_ROW))
    history = [past_rates[:, position] for position in range(2 * SUB)]
    membrane_voltage = potential
    for instant in range(OUTER * SUB):
        spiking_rates = jnp.tanh(membrane_voltage).astype(jnp.bfloat16)
        selected_rows = jnp.take_along_axis(spiking_rates, delay_table, axis=2)
        stacked = jnp.stack(history, axis=1)
        forward = incoming(stacked, 1, delays[:, 0], ff_weight, instant)
        backward = incoming(stacked, -1, delays[:, 1], fb_weight, instant)
        history.append(selected_rows)
        recurrent_drive = lax.map(lambda product_factors: jnp.dot(product_factors[0], product_factors[1], preferred_element_type=jnp.float32), (spiking_rates, recurrence))
        membrane_voltage = membrane_voltage + leak_rate[:, None, :] * (-membrane_voltage + recurrent_drive + forward + backward + stimulus)
    return membrane_voltage
```

```python
import functools

import jax
import jax.numpy as jnp
from jax import lax
from jax.experimental import pallas as pl
from jax.experimental.pallas import tpu as pltpu
from jax.sharding import PartitionSpec as P

SUB = 3
OUTER = 2
BF16 = jnp.bfloat16
F32 = jnp.float32
VMEM_SPEC = pl.BlockSpec(memory_space=pltpu.VMEM)
SMEM_SPEC = pl.BlockSpec(memory_space=pltpu.SMEM)
ANY_SPEC = pl.BlockSpec(memory_space=pl.ANY)
PARAMS = pltpu.CompilerParams(vmem_limit_bytes=8 * 1024 * 1024)


def dot(a, b):
    return jnp.dot(a, b, preferred_element_type=F32)


def resident(value):
    return pltpu.with_memory_space_constraint(value, pltpu.VMEM)


def cost(flops, read):
    return pl.CostEstimate(flops=flops, bytes_accessed=read, transcendentals=0)


def shifted(value, axis, steps):
    count = lax.axis_size(axis)
    pairs = [(source, (source + steps) % count) for source in range(count)]
    return lax.ppermute(value, axis, pairs)


def tile_of(columns):
    return 512 if columns % 512 == 0 else columns


def first_rates_kernel(potential_ref, rates_ref):
    rates_ref[...] = jnp.tanh(potential_ref[...]).astype(BF16)


def select_kernel(index_ref, select_ref):
    neurons, chosen = select_ref.shape
    rows = lax.broadcasted_iota(jnp.int32, (neurons, chosen), 0)
    select_ref[...] = jnp.where(rows == index_ref[...], 1.0, 0.0).astype(BF16)


def loaded_tiles(weight_ref, first_row, kept_ref, sems, tile, step):
    depth, columns = kept_ref.shape
    count = columns // tile

    def copy(n):
        span = pl.ds(n * tile, tile)
        return pltpu.make_async_copy(
            weight_ref.at[pl.ds(first_row, depth), span], kept_ref.at[:, span], sems.at[n]
        )

    for n in range(count):
        copy(n).start()
    for n in range(count):
        copy(n).wait()
        step(n * tile)


def first_own_kernel(block_ref, rates_ref, weight_ref, stimulus_ref, kept_ref, partial_ref, sems, *, tile):
    depth = kept_ref.shape[0]

    def step(start):
        span = pl.ds(start, tile)
        partial_ref[:, span] = stimulus_ref[:, span] + dot(rates_ref[...], kept_ref[:, span])

    first_row = pl.multiple_of(block_ref[0] * depth, depth)
    loaded_tiles(weight_ref, first_row, kept_ref, sems, tile, step)


def updated(potential, leak, drive):
    return potential + leak * (drive - potential)


def first_other_kernel(
    block_ref, rates_ref, weight_ref, partial_ref, potential_ref, leak_ref,
    kept_ref, new_ref, new_rates_ref, sems, *, tile
):
    depth = kept_ref.shape[0]

    def step(start):
        span = pl.ds(start, tile)
        drive = partial_ref[:, span] + dot(rates_ref[...], kept_ref[:, span])
        new = updated(potential_ref[:, span], leak_ref[:, span], drive)
        new_ref[:, span] = new
        new_rates_ref[:, span] = jnp.tanh(new).astype(BF16)

    first_row = pl.multiple_of((1 - block_ref[0]) * depth, depth)
    loaded_tiles(weight_ref, first_row, kept_ref, sems, tile, step)


def arrived(delays_ref, which, instant, past_ref, recent_ref):
    past = past_ref.shape[0]
    position = instant + past - delays_ref[which]
    value = past_ref[jnp.minimum(position, past - 1)]
    if recent_ref is None:
        return value
    later = recent_ref[jnp.clip(position - past, 0, recent_ref.shape[0] - 1)]
    return jnp.where(position < past, value, later)


def maps_kernel(delays_ref, ahead_ref, behind_ref, forward_ref, backward_ref, base_ref, out_ref, *, instant, tile):
    ahead = arrived(delays_ref, 0, instant, ahead_ref, None)
    behind = arrived(delays_ref, 1, instant, behind_ref, None)
    for start in range(0, out_ref.shape[1], tile):
        span = pl.ds(start, tile)
        out_ref[:, span] = (
            base_ref[:, span] + dot(ahead, forward_ref[:, span]) + dot(behind, backward_ref[:, span])
        )


def own_kernel(*refs, instant, tile, late, project):
    refs = list(refs)
    delays_ref, rates_ref, weight_ref, stimulus_ref = refs[:4]
    forward_ref, backward_ref, ahead_ref, behind_ref = refs[4:8]
    refs = refs[8:]
    recent_ahead_ref = recent_behind_ref = None
    if late:
        recent_ahead_ref, recent_behind_ref = refs[:2]
        refs = refs[2:]
    if project:
        select_ref, partial_ref, chosen_ref = refs
        chosen_ref[...] = dot(rates_ref[...], select_ref[...]).astype(BF16)
    else:
        (partial_ref,) = refs
    ahead = arrived(delays_ref, 0, instant, ahead_ref, recent_ahead_ref)
    behind = arrived(delays_ref, 1, instant, behind_ref, recent_behind_ref)
    for start in range(0, partial_ref.shape[1], tile):
        span = pl.ds(start, tile)
        partial_ref[:, span] = (
            stimulus_ref[:, span]
            + dot(ahead, forward_ref[:, span])
            + dot(behind, backward_ref[:, span])
            + dot(rates_ref[...], weight_ref[:, span])
        )


def other_kernel(rates_ref, weight_ref, partial_ref, potential_ref, leak_ref, new_ref, new_rates_ref, *, tile):
    for start in range(0, new_ref.shape[1], tile):
        span = pl.ds(start, tile)
        drive = partial_ref[:, span] + dot(rates_ref[...], weight_ref[:, span])
        new = updated(potential_ref[:, span], leak_ref[:, span], drive)
        new_ref[:, span] = new
        new_rates_ref[:, span] = jnp.tanh(new).astype(BF16)


def last_kernel(rates_ref, weight_ref, partial_ref, potential_ref, leak_ref, new_ref, *, tile):
    for start in range(0, new_ref.shape[1], tile):
        span = pl.ds(start, tile)
        drive = partial_ref[:, span] + dot(rates_ref[...], weight_ref[:, span])
        new_ref[:, span] = updated(potential_ref[:, span], leak_ref[:, span], drive)


def local(
    proj_index, delays, past_rates, potential, stimulus, leak_rate, recurrence, ff_weight, fb_weight
):
    index, lags, past = proj_index, delays[0], past_rates[0]
    weight = pltpu.with_memory_space_constraint(recurrence[0], pltpu.HBM)
    x = resident(potential[0])
    stimulus = resident(stimulus[0])
    leak = resident(leak_rate)
    forward, backward = resident(ff_weight[0]), resident(fb_weight[0])
    block = lax.axis_index("row").astype(jnp.int32)[None]
    trials, columns = potential.shape[1:]
    chosen = index.shape[1]
    depth = weight.shape[0] // lax.axis_size("row")
    tile = tile_of(columns)
    wide = pltpu.VMEM((trials, columns), F32)
    narrow = pltpu.VMEM((trials, columns), BF16)
    kept = pltpu.VMEM((depth, columns), BF16)
    flops = 2 * trials * depth * columns
    read = depth * columns * 2
    sems = [pltpu.SemaphoreType.DMA((columns // tile,))]

    def call(kernel, outs, in_specs, scratch=(), estimate=None, **static):
        many = isinstance(outs, tuple)
        return pl.pallas_call(
            functools.partial(kernel, **static) if static else kernel,
            out_shape=outs,
            in_specs=in_specs,
            out_specs=tuple(VMEM_SPEC for _ in outs) if many else VMEM_SPEC,
            scratch_shapes=list(scratch),
            compiler_params=PARAMS,
            cost_estimate=estimate,
            name=kernel.__name__,
        )

    rates = call(first_rates_kernel, narrow, [VMEM_SPEC])(x)
    select = call(select_kernel, pltpu.VMEM((columns, chosen), BF16), [VMEM_SPEC])(resident(index))
    other_rates = shifted(rates, "row", 1)
    past_ahead = shifted(past, "area", 1)
    past_behind = shifted(past, "area", -1)
    own_weight, partial = call(
        first_own_kernel, (kept, wide),
        [SMEM_SPEC, VMEM_SPEC, ANY_SPEC, VMEM_SPEC], sems, cost(flops, read), tile=tile,
    )(block, resident(rates), weight, stimulus)
    own_weight = resident(own_weight)
    past_ahead, past_behind = resident(past_ahead), resident(past_behind)
    partial = call(
        maps_kernel, wide, [SMEM_SPEC] + [VMEM_SPEC] * 5, instant=0, tile=tile
    )(lags, past_ahead, past_behind, forward, backward, resident(partial))
    other_weight, x, new_rates = call(
        first_other_kernel, (kept, wide, narrow),
        [SMEM_SPEC, VMEM_SPEC, ANY_SPEC] + [VMEM_SPEC] * 3, sems, cost(flops, read), tile=tile,
    )(block, resident(other_rates), weight, resident(partial), x, leak)
    other_weight = resident(other_weight)
    picks = [call(pick_kernel, pltpu.VMEM((trials, chosen), BF16), [VMEM_SPEC] * 2)(resident(rates), resident(select))]
    recent = ()
    steps = SUB * OUTER
    for instant in range(1, steps):
        rates, x = resident(new_rates), resident(x)
        other_rates = resident(shifted(new_rates, "row", 1))
        project = instant < SUB
        late = instant >= SUB
        extra = [resident(select)] if project else []
        outs = (wide, pltpu.VMEM((trials, chosen), BF16)) if project else wide
        partial = call(
            own_kernel, outs, [SMEM_SPEC] + [VMEM_SPEC] * (7 + len(recent) + len(extra)),
            (), cost(flops, read), instant=instant, tile=tile, late=late, project=project,
        )(lags, rates, own_weight, stimulus, forward, backward, past_ahead, past_behind, *recent, *extra)
        if project:
            partial, pick = partial
            picks.append(pick)
            if instant + 1 == SUB:
                block_rates = jnp.stack(picks, axis=0)
                recent = (
                    resident(shifted(block_rates, "area", 1)),
                    resident(shifted(block_rates, "area", -1)),
                )
        arguments = (other_rates, other_weight, resident(partial), x, leak)
        if instant + 1 == steps:
            x = call(last_kernel, jax.ShapeDtypeStruct((trials, columns), F32), [VMEM_SPEC] * 5, tile=tile)(*arguments)
        else:
            x, new_rates = call(
                other_kernel, (wide, narrow), [VMEM_SPEC] * 5, (), cost(flops, read), tile=tile
            )(*arguments)
    return x[None]


def pick_kernel(rates_ref, select_ref, chosen_ref):
    chosen_ref[...] = dot(rates_ref[...], select_ref[...]).astype(BF16)


def solution(mesh):
    return jax.shard_map(
        local,
        mesh=mesh,
        in_specs=(
            P("area", "row"),
            P("area", None),
            P("area", None, "groups", "row"),
            P("area", "groups", "row"),
            P("area", "groups", "row"),
            P("area", "row"),
            P("area", None, "row"),
            P("area", None, "row"),
            P("area", None, "row"),
        ),
        out_specs=P("area", "groups", "row"),
        check_vma=False,
    )
```

```python
import functools

import jax
import jax.numpy as jnp
from jax import lax
from jax.experimental import pallas as pl
from jax.experimental.pallas import tpu as pltpu
from jax.sharding import PartitionSpec as P

SUB = 3
OUTER = 2
SLOTS = OUTER * SUB
BF16 = jnp.bfloat16
F32 = jnp.float32
VMEM_SPEC = pl.BlockSpec(memory_space=pltpu.VMEM)
SMEM_SPEC = pl.BlockSpec(memory_space=pltpu.SMEM)
ANY_SPEC = pl.BlockSpec(memory_space=pl.ANY)
PARAMS = pltpu.CompilerParams(vmem_limit_bytes=8 * 1024 * 1024)


def resident(value):
    return pltpu.with_memory_space_constraint(value, pltpu.VMEM)


def remote(value):
    return pltpu.with_memory_space_constraint(value, pltpu.HBM)


def shifted(value, axis, steps):
    count = lax.axis_size(axis)
    pairs = [(source, (source + steps) % count) for source in range(count)]
    return lax.ppermute(value, axis, pairs)


def largest_tile(size, most):
    return most if size % most == 0 else size


def dot(a, b):
    rows = a.shape[0]
    if rows < 128:
        a = jnp.concatenate([a, jnp.zeros((128 - rows, a.shape[1]), a.dtype)], axis=0)
    return jnp.dot(a, b, preferred_element_type=F32)[:rows]


def updated(potential, leak, drive):
    return potential + leak * (drive - potential)


def first_kernel(
    block_ref, potential_ref, past_ref, weight_ref, kept_potential_ref, rates_ref, packed_ref, kept_ref,
    past_scratch, sems
):
    quarter = kept_ref.shape[0]
    depth = rates_ref.shape[1]
    used = past_scratch.shape[0]
    first_row = pl.multiple_of(block_ref[0] * depth, depth)
    copies = [
        pltpu.make_async_copy(potential_ref, kept_potential_ref, sems.at[0]),
        pltpu.make_async_copy(past_ref.at[pl.ds(past_ref.shape[0] - used, used)], past_scratch, sems.at[1]),
        pltpu.make_async_copy(weight_ref.at[pl.ds(first_row, quarter)], kept_ref, sems.at[2]),
    ]
    for copy in copies:
        copy.start()
    copies[0].wait()
    rates_ref[...] = jnp.tanh(kept_potential_ref[...]).astype(BF16)
    copies[1].wait()
    packed_ref[...] = jnp.concatenate([past_scratch[n] for n in range(used)], axis=1)
    copies[2].wait()


def load_kernel(
    block_ref, rates_ref, other_rates_ref, first_ref, weight_ref, index_ref,
    kept_ref, partial_ref, select_ref, pick_ref, sems, *, chunk, tile
):
    depth = rates_ref.shape[1]
    quarter = first_ref.shape[0]
    own = pl.multiple_of(block_ref[0] * depth, depth)
    other = pl.multiple_of((1 - block_ref[0]) * depth, depth)
    copies = []
    for n in range(kept_ref.shape[0] // chunk):
        at = n * chunk
        row = own + quarter + at if at < depth - quarter else other + at - (depth - quarter)
        copies.append(
            pltpu.make_async_copy(
                weight_ref.at[pl.ds(pl.multiple_of(row, chunk), chunk)], kept_ref.at[pl.ds(at, chunk)], sems.at[n]
            )
        )
    for copy in copies:
        copy.start()
    columns = partial_ref.shape[1]
    rows = lax.broadcasted_iota(jnp.int32, select_ref.shape, 0)
    select_ref[...] = jnp.where(rows == index_ref[...], 1.0, 0.0).astype(BF16)
    for start in range(0, columns, tile):
        span = pl.ds(start, tile)
        partial_ref[:, span] = dot(rates_ref[:, pl.ds(0, quarter)], first_ref[:, span])
    pick_ref[...] = dot(rates_ref[...], select_ref[...]).astype(BF16)
    for n, copy in enumerate(copies):
        copy.wait()
        at = n * chunk
        if at < depth - quarter:
            left = rates_ref[:, pl.ds(quarter + at, chunk)]
        else:
            left = other_rates_ref[:, pl.ds(at - (depth - quarter), chunk)]
        for start in range(0, columns, tile):
            span = pl.ds(start, tile)
            partial_ref[:, span] = partial_ref[:, span] + dot(left, kept_ref[pl.ds(at, chunk), span])


def arrived(delay, instant, past_ref, recent_ref, chosen):
    used = past_ref.shape[1] // chosen
    value = None
    for lag in range(SUB, 2 * SUB):
        position = instant - lag
        if position < 0:
            here = past_ref[:, pl.ds((used + position) * chosen, chosen)]
        else:
            here = recent_ref[:, pl.ds(position * chosen, chosen)]
        value = here if value is None else jnp.where(delay == lag, here, value)
    return value


def batch(delays_ref, which, instants, past_ref, recent_ref, chosen):
    delay = delays_ref[0, which]
    return jnp.concatenate([arrived(delay, n, past_ref, recent_ref, chosen) for n in instants], axis=0)


def finish_kernel(
    delays_ref, partial_ref, potential_ref, leak_ref, stimulus_ref, forward_ref, backward_ref,
    ahead_ref, behind_ref, rates_ref, select_ref, new_ref, new_rates_ref, pick_ref, drives_ref, *, tile
):
    del rates_ref
    trials, columns = new_ref.shape
    chosen = forward_ref.shape[0]
    ahead = batch(delays_ref, 0, range(SUB), ahead_ref, None, chosen)
    behind = batch(delays_ref, 1, range(SUB), behind_ref, None, chosen)
    for start in range(0, columns, tile):
        span = pl.ds(start, tile)
        drives = dot(ahead, forward_ref[:, span]) + dot(behind, backward_ref[:, span])
        stimulus = stimulus_ref[:, span]
        drive = partial_ref[:, span] + drives[:trials] + stimulus
        new = updated(potential_ref[:, span], leak_ref[:, span], drive)
        new_ref[:, span] = new
        new_rates_ref[:, span] = jnp.tanh(new).astype(BF16)
        for n in range(1, SUB):
            drives_ref[n - 1, :, span] = drives[n * trials:(n + 1) * trials] + stimulus
    pick_ref[...] = dot(new_rates_ref[...], select_ref[...]).astype(BF16)


def own_kernel(rates_ref, first_ref, kept_ref, drives_ref, partial_ref, *, tile, which):
    quarter = first_ref.shape[0]
    rest = rates_ref.shape[1] - quarter
    for start in range(0, partial_ref.shape[1], tile):
        span = pl.ds(start, tile)
        partial_ref[:, span] = (
            drives_ref[which, :, span]
            + dot(rates_ref[:, pl.ds(0, quarter)], first_ref[:, span])
            + dot(rates_ref[:, pl.ds(quarter, rest)], kept_ref[pl.ds(0, rest), span])
        )


def other_kernel(other_rates_ref, kept_ref, partial_ref, potential_ref, leak_ref, *refs, tile, pick):
    if pick:
        early_ref, late_ref, select_ref, new_ref, new_rates_ref, block_ref = refs
    else:
        new_ref, new_rates_ref = refs
    depth = other_rates_ref.shape[1]
    rest = kept_ref.shape[0] - depth
    rates = other_rates_ref[...]
    for start in range(0, new_ref.shape[1], tile):
        span = pl.ds(start, tile)
        drive = partial_ref[:, span] + dot(rates, kept_ref[pl.ds(rest, depth), span])
        new = updated(potential_ref[:, span], leak_ref[:, span], drive)
        new_ref[:, span] = new
        new_rates_ref[:, span] = jnp.tanh(new).astype(BF16)
    if pick:
        latest = dot(new_rates_ref[...], select_ref[...]).astype(BF16)
        block_ref[...] = jnp.concatenate([early_ref[...], late_ref[...], latest], axis=1)


def drives_kernel(
    delays_ref, stimulus_ref, forward_ref, backward_ref, ahead_ref, behind_ref, recent_ahead_ref, recent_behind_ref,
    drives_ref, *, tile
):
    trials, columns = stimulus_ref.shape
    chosen = forward_ref.shape[0]
    ahead = batch(delays_ref, 0, range(SUB, 2 * SUB), ahead_ref, recent_ahead_ref, chosen)
    behind = batch(delays_ref, 1, range(SUB, 2 * SUB), behind_ref, recent_behind_ref, chosen)
    for start in range(0, columns, tile):
        span = pl.ds(start, tile)
        drives = dot(ahead, forward_ref[:, span]) + dot(behind, backward_ref[:, span])
        stimulus = stimulus_ref[:, span]
        for n in range(SUB):
            drives_ref[n, :, span] = drives[n * trials:(n + 1) * trials] + stimulus


def last_kernel(other_rates_ref, kept_ref, partial_ref, potential_ref, leak_ref, new_ref, scratch, sems, *, tile):
    depth = other_rates_ref.shape[1]
    rest = kept_ref.shape[0] - depth
    rates = other_rates_ref[...]
    copies = []
    for n, start in enumerate(range(0, new_ref.shape[1], tile)):
        span = pl.ds(start, tile)
        drive = partial_ref[:, span] + dot(rates, kept_ref[pl.ds(rest, depth), span])
        scratch[:, span] = updated(potential_ref[:, span], leak_ref[:, span], drive)
        copies.append(pltpu.make_async_copy(scratch.at[:, span], new_ref.at[:, span], sems.at[n]))
        copies[-1].start()
    for copy in copies:
        copy.wait()


def call(kernel, outs, in_specs, scratch=(), out_specs=None, **static):
    many = isinstance(outs, tuple)
    return pl.pallas_call(
        functools.partial(kernel, **static) if static else kernel,
        out_shape=outs,
        in_specs=in_specs,
        out_specs=out_specs or (tuple(VMEM_SPEC for _ in outs) if many else VMEM_SPEC),
        scratch_shapes=list(scratch),
        compiler_params=PARAMS,
        name=kernel.__name__,
    )


def local(
    proj_index, delays, past_rates, potential, stimulus, leak_rate, recurrence, ff_weight, fb_weight
):
    weight = remote(recurrence[0])
    stimulus, leak = resident(stimulus[0]), resident(leak_rate)
    forward, backward = resident(ff_weight[0]), resident(fb_weight[0])
    block = lax.axis_index("row").astype(jnp.int32)[None]
    trials, columns = potential.shape[1:]
    chosen = proj_index.shape[1]
    depth = columns
    quarter = depth // 2
    rest = weight.shape[0] - quarter
    used = past_rates.shape[1] - 1
    chunk = largest_tile(quarter, 512)
    tile = largest_tile(columns, 1024)
    small = largest_tile(columns, 512)
    wide = pltpu.VMEM((trials, columns), F32)
    narrow = pltpu.VMEM((trials, columns), BF16)
    picked = pltpu.VMEM((trials, chosen), BF16)
    copies = pltpu.SemaphoreType.DMA

    x, rates, packed, first_weight = call(
        first_kernel,
        (wide, narrow, pltpu.VMEM((trials, used * chosen), BF16), pltpu.VMEM((quarter, columns), BF16)),
        [SMEM_SPEC] + [ANY_SPEC] * 3,
        [pltpu.VMEM((used, trials, chosen), BF16), copies((3,))],
    )(block, remote(potential[0]), remote(past_rates[0]), weight)
    first_weight = resident(first_weight)
    other_rates = resident(shifted(rates, "row", 1))
    ahead = resident(shifted(packed, "area", 1))
    behind = resident(shifted(packed, "area", -1))
    kept, partial, select, pick_early = call(
        load_kernel,
        (pltpu.VMEM((rest, columns), BF16), wide, pltpu.VMEM((depth, chosen), BF16), picked),
        [SMEM_SPEC] + [VMEM_SPEC] * 3 + [ANY_SPEC, VMEM_SPEC],
        [copies((rest // chunk,))], chunk=chunk, tile=tile,
    )(block, resident(rates), other_rates, first_weight, weight, resident(proj_index))
    kept, select = resident(kept), resident(select)
    x, rates, pick_late, drives = call(
        finish_kernel, (wide, narrow, picked, pltpu.VMEM((SUB - 1, trials, columns), F32)),
        [SMEM_SPEC] + [VMEM_SPEC] * 10, tile=small,
    )(
        delays, resident(partial), resident(x), leak, stimulus, forward, backward, ahead, behind,
        resident(rates), select,
    )
    which = 0
    for instant in range(1, SLOTS):
        other_rates = resident(shifted(rates, "row", 1))
        if instant == SUB:
            drives = call(
                drives_kernel, pltpu.VMEM((SUB, trials, columns), F32), [SMEM_SPEC] + [VMEM_SPEC] * 7, tile=small
            )(delays, stimulus, forward, backward, ahead, behind, recent_ahead, recent_behind)
            which = 0
        partial = call(own_kernel, wide, [VMEM_SPEC] * 4, tile=tile, which=which)(
            resident(rates), first_weight, kept, resident(drives)
        )
        which += 1
        arguments = (other_rates, kept, resident(partial), resident(x), leak)
        if instant + 1 == SLOTS:
            return call(
                last_kernel, jax.ShapeDtypeStruct((trials, columns), F32), [VMEM_SPEC] * 5,
                [pltpu.VMEM((trials, columns), F32), copies((columns // small,))], ANY_SPEC, tile=small,
            )(*arguments)[None]
        if instant + 1 == SUB - 1:
            x, rates, picks = call(
                other_kernel, (wide, narrow, pltpu.VMEM((trials, SUB * chosen), BF16)), [VMEM_SPEC] * 8,
                tile=small, pick=True,
            )(*arguments, resident(pick_early), resident(pick_late), select)
            recent_ahead = resident(shifted(picks, "area", 1))
            recent_behind = resident(shifted(picks, "area", -1))
        else:
            x, rates = call(other_kernel, (wide, narrow), [VMEM_SPEC] * 5, tile=small, pick=False)(*arguments)


def solution(mesh):
    return jax.shard_map(
        local,
        mesh=mesh,
        in_specs=(
            P("area", "row"),
            P("area", None),
            P("area", None, "groups", "row"),
            P("area", "groups", "row"),
            P("area", "groups", "row"),
            P("area", "row"),
            P("area", None, "row"),
            P("area", None, "row"),
            P("area", None, "row"),
        ),
        out_specs=P("area", "groups", "row"),
        check_vma=False,
    )
```

```python
import functools

import jax
import jax.numpy as jnp
from jax import lax
from jax.experimental import pallas as pl
from jax.experimental.pallas import tpu as pltpu
from jax.sharding import PartitionSpec as P

SUB = 3
OUTER = 2
SLOTS = OUTER * SUB
BF16 = jnp.bfloat16
F32 = jnp.float32
VMEM_SPEC = pl.BlockSpec(memory_space=pltpu.VMEM)
SMEM_SPEC = pl.BlockSpec(memory_space=pltpu.SMEM)
ANY_SPEC = pl.BlockSpec(memory_space=pl.ANY)
PARAMS = pltpu.CompilerParams(vmem_limit_bytes=8 * 1024 * 1024)


def resident(value):
    return pltpu.with_memory_space_constraint(value, pltpu.VMEM)


def remote(value):
    return pltpu.with_memory_space_constraint(value, pltpu.HBM)


def swapped(value, axis, parity):
    count = lax.axis_size(axis)
    pairs = [(source, (source + (1 if source % 2 == parity else -1)) % count) for source in range(count)]
    return lax.ppermute(value, axis, pairs)


def largest_tile(size, most):
    return most if size % most == 0 else size


def dot(a, b):
    rows = a.shape[0]
    if rows < 128:
        a = jnp.concatenate([a, jnp.zeros((128 - rows, a.shape[1]), a.dtype)], axis=0)
    return jnp.dot(a, b, preferred_element_type=F32)[:rows]


def picked(rates_ref, select_ref):
    return dot(rates_ref[...], select_ref[...]).astype(BF16)


def updated(potential, leak, drive):
    return potential + leak * (drive - potential)


def first_kernel(
    potential_ref, past_ref, weight_ref,
    kept_potential_ref, rates_ref, packed_ref, kept_ref, past_scratch, sems
):
    quarter = kept_ref.shape[0]
    depth = rates_ref.shape[1]
    used = past_scratch.shape[0]
    first_row = pl.multiple_of(lax.axis_index("row") * depth, depth)
    copies = [
        pltpu.make_async_copy(potential_ref, kept_potential_ref, sems.at[0]),
        pltpu.make_async_copy(past_ref.at[pl.ds(past_ref.shape[0] - used, used)], past_scratch, sems.at[1]),
        pltpu.make_async_copy(weight_ref.at[pl.ds(first_row, quarter)], kept_ref, sems.at[2]),
    ]
    for copy in copies:
        copy.start()
    copies[0].wait()
    rates_ref[...] = jnp.tanh(kept_potential_ref[...]).astype(BF16)
    copies[1].wait()
    packed_ref[...] = jnp.concatenate([past_scratch[n] for n in range(used)], axis=1)
    copies[2].wait()


def load_kernel(
    rates_ref, other_rates_ref, first_ref, index_ref, weight_ref,
    kept_ref, partial_ref, select_ref, pick_ref, sems, *, chunk, tile
):
    depth = rates_ref.shape[1]
    quarter = first_ref.shape[0]
    block = lax.axis_index("row")
    own = pl.multiple_of(block * depth, depth)
    other = pl.multiple_of((1 - block) * depth, depth)
    copies = []
    for n in range(kept_ref.shape[0] // chunk):
        at = n * chunk
        row = own + quarter + at if at < depth - quarter else other + at - (depth - quarter)
        copies.append(
            pltpu.make_async_copy(
                weight_ref.at[pl.ds(pl.multiple_of(row, chunk), chunk)], kept_ref.at[pl.ds(at, chunk)], sems.at[n]
            )
        )
    for copy in copies:
        copy.start()
    columns = partial_ref.shape[1]
    for start in range(0, columns, tile):
        span = pl.ds(start, tile)
        partial_ref[:, span] = dot(rates_ref[:, pl.ds(0, quarter)], first_ref[:, span])
    rows = lax.broadcasted_iota(jnp.int32, select_ref.shape, 0)
    select_ref[...] = jnp.where(rows == index_ref[...], 1.0, 0.0).astype(BF16)
    pick_ref[...] = picked(rates_ref, select_ref)
    for n, copy in enumerate(copies):
        copy.wait()
        at = n * chunk
        if at < depth - quarter:
            left = rates_ref[:, pl.ds(quarter + at, chunk)]
        else:
            left = other_rates_ref[:, pl.ds(at - (depth - quarter), chunk)]
        for start in range(0, columns, tile):
            span = pl.ds(start, tile)
            partial_ref[:, span] = partial_ref[:, span] + dot(left, kept_ref[pl.ds(at, chunk), span])


def arrived(delay, instant, past, recent, chosen):
    used = past.shape[1] // chosen
    value = None
    for lag in range(SUB, 2 * SUB):
        place = instant - lag
        if place < 0:
            here = past[:, (used + place) * chosen:(used + place + 1) * chosen]
        else:
            here = recent[:, place * chosen:(place + 1) * chosen]
        value = here if value is None else jnp.where(delay == lag, here, value)
    return value


def mapped(delays_ref, instants, past_refs, recent_refs, forward_ref, backward_ref, stimulus_ref, tile):
    trials, columns = stimulus_ref.shape
    chosen = forward_ref.shape[0]
    odd = lax.axis_index("area") % 2 == 1
    sides = []
    for which in range(2):
        first = odd if which == 0 else jnp.logical_not(odd)
        past, recent = (
            jnp.where(first, refs[0][...], refs[1][...]) if refs else None for refs in (past_refs, recent_refs)
        )
        delay = delays_ref[0, which]
        sides.append(jnp.concatenate([arrived(delay, n, past, recent, chosen) for n in instants], axis=0))
    both = jnp.concatenate(sides, axis=1)
    for start in range(0, columns, tile):
        span = pl.ds(start, tile)
        maps = jnp.concatenate([forward_ref[:, span], backward_ref[:, span]], axis=0)
        drives = dot(both, maps)
        stimulus = stimulus_ref[:, span]
        yield span, [drives[n * trials:(n + 1) * trials] + stimulus for n in range(len(instants))]


def finish_kernel(
    delays_ref, partial_ref, potential_ref, leak_ref, stimulus_ref, forward_ref, backward_ref,
    even_ref, odd_ref, new_ref, new_rates_ref, drives_ref, *, tile
):
    inputs = mapped(
        delays_ref, range(SUB), (even_ref, odd_ref), (), forward_ref, backward_ref, stimulus_ref, tile
    )
    for span, (drive, *later) in inputs:
        new = updated(potential_ref[:, span], leak_ref[:, span], partial_ref[:, span] + drive)
        new_ref[:, span] = new
        new_rates_ref[:, span] = jnp.tanh(new).astype(BF16)
        for n, drive in enumerate(later):
            drives_ref[n, :, span] = drive


def drives_kernel(
    delays_ref, stimulus_ref, forward_ref, backward_ref, *refs, tile
):
    even_ref, odd_ref, recent_even_ref, recent_odd_ref, after_ref, drives_ref = refs
    del after_ref
    inputs = mapped(
        delays_ref, range(SUB, SLOTS), (even_ref, odd_ref), (recent_even_ref, recent_odd_ref),
        forward_ref, backward_ref, stimulus_ref, tile
    )
    for span, drives in inputs:
        for n, drive in enumerate(drives):
            drives_ref[n, :, span] = drive


def own_kernel(rates_ref, first_ref, kept_ref, *refs, tile, pick):
    if pick:
        select_ref, partial_ref, pick_ref = refs
        pick_ref[...] = picked(rates_ref, select_ref)
    else:
        (partial_ref,) = refs
    quarter = first_ref.shape[0]
    rest = rates_ref.shape[1] - quarter
    for start in range(0, partial_ref.shape[1], tile):
        span = pl.ds(start, tile)
        partial_ref[:, span] = (
            dot(rates_ref[:, pl.ds(0, quarter)], first_ref[:, span])
            + dot(rates_ref[:, pl.ds(quarter, rest)], kept_ref[pl.ds(0, rest), span])
        )


def other_kernel(other_rates_ref, kept_ref, partial_ref, drives_ref, potential_ref, leak_ref, *refs, tile, which, pick):
    if pick:
        select_ref, early_ref, middle_ref, new_ref, new_rates_ref, block_ref = refs
    else:
        new_ref, new_rates_ref = refs
    depth = other_rates_ref.shape[1]
    rest = kept_ref.shape[0] - depth
    rates = other_rates_ref[...]
    for start in range(0, new_ref.shape[1], tile):
        span = pl.ds(start, tile)
        drive = partial_ref[:, span] + drives_ref[which, :, span] + dot(rates, kept_ref[pl.ds(rest, depth), span])
        new = updated(potential_ref[:, span], leak_ref[:, span], drive)
        new_ref[:, span] = new
        new_rates_ref[:, span] = jnp.tanh(new).astype(BF16)
    if pick:
        latest = picked(new_rates_ref, select_ref)
        block_ref[...] = jnp.concatenate([early_ref[...], middle_ref[...], latest], axis=1)


def last_kernel(
    other_rates_ref, kept_ref, partial_ref, drives_ref, potential_ref, leak_ref, new_ref, scratch, sems, *, tile, which
):
    depth = other_rates_ref.shape[1]
    rest = kept_ref.shape[0] - depth
    rates = other_rates_ref[...]
    copies = []
    for n, start in enumerate(range(0, new_ref.shape[1], tile)):
        span = pl.ds(start, tile)
        drive = partial_ref[:, span] + drives_ref[which, :, span] + dot(rates, kept_ref[pl.ds(rest, depth), span])
        scratch[:, span] = updated(potential_ref[:, span], leak_ref[:, span], drive)
        copies.append(pltpu.make_async_copy(scratch.at[:, span], new_ref.at[:, span], sems.at[n]))
        copies[-1].start()
    for copy in copies:
        copy.wait()


def call(kernel, outs, in_specs, scratch=(), out_specs=None, estimate=None, **static):
    many = isinstance(outs, tuple)
    return pl.pallas_call(
        functools.partial(kernel, **static) if static else kernel,
        out_shape=outs,
        in_specs=in_specs,
        out_specs=out_specs or (tuple(VMEM_SPEC for _ in outs) if many else VMEM_SPEC),
        scratch_shapes=list(scratch),
        compiler_params=PARAMS,
        cost_estimate=estimate and pl.CostEstimate(flops=estimate, bytes_accessed=0, transcendentals=0),
        name=kernel.__name__,
    )


COST_OWN = 5_000_000_000
COST_OTHER = None
DRIVE_TILE = 1024


def local(
    proj_index, delays, past_rates, potential, stimulus, leak_rate, recurrence, ff_weight, fb_weight
):
    weight = remote(recurrence[0])
    stimulus, leak = resident(stimulus[0]), resident(leak_rate)
    forward, backward = resident(ff_weight[0]), resident(fb_weight[0])
    trials, columns = potential.shape[1:]
    chosen = proj_index.shape[1]
    depth = columns
    quarter = depth // 2
    rest = weight.shape[0] - quarter
    used = past_rates.shape[1] - 1
    chunk = largest_tile(quarter, 512)
    tile = largest_tile(columns, 1024)
    small = largest_tile(columns, 512)
    wide = pltpu.VMEM((trials, columns), F32)
    narrow = pltpu.VMEM((trials, columns), BF16)
    pick = pltpu.VMEM((trials, chosen), BF16)
    copies = pltpu.SemaphoreType.DMA

    def around(value):
        odd = resident(swapped(value, "area", 1))
        return resident(swapped(value, "area", 0)), odd

    x, rates, packed, first_weight = call(
        first_kernel,
        (wide, narrow, pltpu.VMEM((trials, used * chosen), BF16), pltpu.VMEM((quarter, columns), BF16)),
        [ANY_SPEC] * 3,
        [pltpu.VMEM((used, trials, chosen), BF16), copies((3,))],
    )(remote(potential[0]), remote(past_rates[0]), weight)
    first_weight = resident(first_weight)
    other_rates = resident(swapped(rates, "row", 0))
    past = around(packed)
    kept, partial, select, early = call(
        load_kernel, (pltpu.VMEM((rest, columns), BF16), wide, pltpu.VMEM((depth, chosen), BF16), pick),
        [VMEM_SPEC] * 4 + [ANY_SPEC],
        [copies((rest // chunk,))], chunk=chunk, tile=tile,
    )(resident(rates), other_rates, first_weight, resident(proj_index), weight)
    kept, select = resident(kept), resident(select)
    maps = (forward, backward)
    x, rates, drives = call(
        finish_kernel, (wide, narrow, pltpu.VMEM((SUB - 1, trials, columns), F32)),
        [SMEM_SPEC] + [VMEM_SPEC] * 8, tile=DRIVE_TILE or columns
    )(delays, resident(partial), resident(x), leak, stimulus, *maps, *past)
    which = 0
    for instant in range(1, SLOTS):
        other_rates = resident(swapped(rates, "row", 0))
        own = (resident(rates), first_weight, kept)
        if instant == 1:
            partial, middle = call(
                own_kernel, (wide, pick), [VMEM_SPEC] * 4, tile=tile, pick=True, estimate=COST_OWN,
            )(*own, select)
        else:
            partial = call(own_kernel, wide, [VMEM_SPEC] * 3, tile=tile, pick=False, estimate=COST_OWN)(*own)
        partial = resident(partial)
        if instant == SUB:
            drives = call(
                drives_kernel, pltpu.VMEM((SUB, trials, columns), F32), [SMEM_SPEC] + [VMEM_SPEC] * 8,
                tile=DRIVE_TILE or columns,
            )(delays, stimulus, *maps, *past, *recent, partial)
            which = 0
        arguments = (other_rates, kept, partial, resident(drives), resident(x), leak)
        if instant + 1 == SLOTS:
            return call(
                last_kernel, jax.ShapeDtypeStruct((trials, columns), F32), [VMEM_SPEC] * 6,
                [pltpu.VMEM((trials, columns), F32), copies((columns // small,))], ANY_SPEC, tile=small, which=which,
            )(*arguments)[None]
        if instant + 1 == SUB - 1:
            x, rates, recent = call(
                other_kernel, (wide, narrow, pltpu.VMEM((trials, SUB * chosen), BF16)), [VMEM_SPEC] * 9,
                tile=small, which=which, pick=True, estimate=COST_OTHER,
            )(*arguments, select, resident(early), resident(middle))
            recent = around(recent)
        else:
            x, rates = call(
                other_kernel, (wide, narrow), [VMEM_SPEC] * 6, tile=small, which=which, pick=False, estimate=COST_OTHER,
            )(*arguments)
        which += 1


def solution(mesh):
    return jax.shard_map(
        local,
        mesh=mesh,
        in_specs=(
            P("area", "row"),
            P("area", None),
            P("area", None, "groups", "row"),
            P("area", "groups", "row"),
            P("area", "groups", "row"),
            P("area", "row"),
            P("area", None, "row"),
            P("area", None, "row"),
            P("area", None, "row"),
        ),
        out_specs=P("area", "groups", "row"),
        check_vma=False,
    )
```

```python
import functools

import jax
import jax.numpy as jnp
from jax import lax
from jax.experimental import pallas as pl
from jax.experimental.pallas import tpu as pltpu
from jax.sharding import PartitionSpec as P

SUB = 3
OUTER = 2
SLOTS = OUTER * SUB
BF16 = jnp.bfloat16
F32 = jnp.float32
VMEM_SPEC = pl.BlockSpec(memory_space=pltpu.VMEM)
SMEM_SPEC = pl.BlockSpec(memory_space=pltpu.SMEM)
ANY_SPEC = pl.BlockSpec(memory_space=pl.ANY)
PARAMS = pltpu.CompilerParams(vmem_limit_bytes=8 * 1024 * 1024)


def resident(value):
    return pltpu.with_memory_space_constraint(value, pltpu.VMEM)


def remote(value):
    return pltpu.with_memory_space_constraint(value, pltpu.HBM)


def swapped(value, axis, parity):
    count = lax.axis_size(axis)
    pairs = [(source, (source + (1 if source % 2 == parity else -1)) % count) for source in range(count)]
    return lax.ppermute(value, axis, pairs)


def largest_tile(size, most):
    return most if size % most == 0 else size


def parts(size):
    return [size // 2] + parts(size // 2) if size % 512 == 0 and size > LEAST else [size]


def packed(slots):
    whole = slots[0].shape[1] // 128 * 128
    pieces = [slot[:, :whole] for slot in slots] if whole else []
    return jnp.concatenate(pieces + ([slot[:, whole:] for slot in slots] if whole < slots[0].shape[1] else []), axis=1)


def unpacked(block, n, chosen):
    whole = chosen // 128 * 128
    left = chosen - whole
    start = block.shape[1] // chosen * whole + n * left
    return block[:, n * whole:(n + 1) * whole], block[:, start:start + left]


def dot(a, b):
    rows = a.shape[0]
    if rows < 128:
        a = jnp.concatenate([a, jnp.zeros((128 - rows, a.shape[1]), a.dtype)], axis=0)
    return jnp.dot(a, b, preferred_element_type=F32)[:rows]


def picked(rates_ref, select_ref):
    return dot(rates_ref[...], select_ref[...]).astype(BF16)


def updated(potential, leak, drive):
    return potential + leak * (drive - potential)


def first_kernel(
    potential_ref, past_ref, kept_potential_ref, rates_ref, packed_ref, past_scratch, sems
):
    used = past_scratch.shape[0]
    copies = [
        pltpu.make_async_copy(potential_ref, kept_potential_ref, sems.at[0]),
        pltpu.make_async_copy(past_ref.at[pl.ds(past_ref.shape[0] - used, used)], past_scratch, sems.at[1]),
    ]
    for copy in copies:
        copy.start()
    copies[0].wait()
    rates_ref[...] = jnp.tanh(kept_potential_ref[...]).astype(BF16)
    copies[1].wait()
    packed_ref[...] = packed([past_scratch[n] for n in range(used)])


def load_kernel(
    rates_ref, other_rates_ref, index_ref, weight_ref,
    kept_ref, partial_ref, select_ref, pick_ref, index_scratch, sems, *, chunks, tile
):
    depth = rates_ref.shape[1]
    block = lax.axis_index("row")
    own = pl.multiple_of(block * depth, depth)
    other = pl.multiple_of((1 - block) * depth, depth)
    index_copy = pltpu.make_async_copy(index_ref, index_scratch, sems.at[len(chunks)])
    index_copy.start()
    copies = []
    for n, (at, size) in enumerate(chunks):
        row = own + at if at < depth else other + at - depth
        copies.append(
            pltpu.make_async_copy(
                weight_ref.at[pl.ds(pl.multiple_of(row, 16), size)], kept_ref.at[pl.ds(at, size)], sems.at[n]
            )
        )
        copies[-1].start()
    columns = partial_ref.shape[1]
    for n, (at, size) in enumerate(chunks):
        if n == 1:
            index_copy.wait()
            rows = lax.broadcasted_iota(jnp.int32, select_ref.shape, 0)
            select_ref[...] = jnp.where(rows == index_scratch[...], 1.0, 0.0).astype(BF16)
            pick_ref[...] = picked(rates_ref, select_ref)
        copies[n].wait()
        left = rates_ref[:, pl.ds(at, size)] if at < depth else other_rates_ref[:, pl.ds(at - depth, size)]
        for start in range(0, columns, tile):
            span = pl.ds(start, tile)
            product = dot(left, kept_ref[pl.ds(at, size), span])
            partial_ref[:, span] = partial_ref[:, span] + product if n else product


def arrived(delay, instant, past, recent, chosen):
    used = past.shape[1] // chosen
    value = None
    for lag in range(SUB, 2 * SUB):
        place = instant - lag
        here = unpacked(past, used + place, chosen) if place < 0 else unpacked(recent, place, chosen)
        value = here if value is None else [jnp.where(delay == lag, new, old) for new, old in zip(here, value)]
    return value


def mapped(delays_ref, instants, past_refs, recent_refs, forward_ref, backward_ref, stimulus_ref, tile):
    trials, columns = stimulus_ref.shape
    chosen = forward_ref.shape[0]
    whole = chosen // 128 * 128
    odd = lax.axis_index("area") % 2 == 1
    pieces = []
    for which in range(2):
        near = odd if which == 0 else jnp.logical_not(odd)
        past = jnp.where(near, past_refs[1][...], past_refs[0][...])
        recent = jnp.where(near, recent_refs[0][...], recent_refs[1][...]) if recent_refs else None
        delay = delays_ref[0, which]
        values = [arrived(delay, n, past, recent, chosen) for n in instants]
        pieces.append([jnp.concatenate(piece, axis=0) for piece in zip(*values)])
    both = jnp.concatenate([pieces[0][0], pieces[1][0], pieces[0][1], pieces[1][1]], axis=1)
    for start in range(0, columns, tile):
        span = pl.ds(start, tile)
        maps = jnp.concatenate(
            [ref[rows, span] for rows in (pl.ds(0, whole), pl.ds(whole, chosen - whole)) for ref in (forward_ref, backward_ref)],
            axis=0,
        )
        drives = dot(both, maps)
        stimulus = stimulus_ref[:, span]
        yield span, [drives[n * trials:(n + 1) * trials] + stimulus for n in range(len(instants))]


def maps_kernel(delays_ref, partial_ref, potential_ref, leak_ref, stimulus_ref, forward_ref, backward_ref, *refs, tile, start):
    *blocks, new_ref, new_rates_ref, drives_ref = refs
    inputs = mapped(
        delays_ref, range(start, start + SUB), blocks[:2], blocks[2:], forward_ref, backward_ref, stimulus_ref, tile
    )
    for span, (drive, *later) in inputs:
        new = updated(potential_ref[:, span], leak_ref[:, span], partial_ref[:, span] + drive)
        new_ref[:, span] = new
        new_rates_ref[:, span] = jnp.tanh(new).astype(BF16)
        for n, drive in enumerate(later):
            drives_ref[n, :, span] = drive


def sum_kernel(other_rates_ref, kept_ref, partial_ref, whole_ref, *, tile):
    depth = other_rates_ref.shape[1]
    rest = kept_ref.shape[0] - depth
    for start in range(0, whole_ref.shape[1], tile):
        span = pl.ds(start, tile)
        whole_ref[:, span] = partial_ref[:, span] + dot(other_rates_ref[...], kept_ref[pl.ds(rest, depth), span])


def own_kernel(rates_ref, kept_ref, *refs, tile, pick):
    if pick:
        select_ref, partial_ref, pick_ref = refs
        pick_ref[...] = picked(rates_ref, select_ref)
    else:
        (partial_ref,) = refs
    depth = rates_ref.shape[1]
    for start in range(0, partial_ref.shape[1], tile):
        span = pl.ds(start, tile)
        partial_ref[:, span] = dot(rates_ref[...], kept_ref[pl.ds(0, depth), span])


def other_kernel(other_rates_ref, kept_ref, partial_ref, drives_ref, potential_ref, leak_ref, *refs, tile, which, pick):
    if pick:
        select_ref, early_ref, middle_ref, new_ref, new_rates_ref, block_ref = refs
    else:
        new_ref, new_rates_ref = refs
    depth = other_rates_ref.shape[1]
    rest = kept_ref.shape[0] - depth
    rates = other_rates_ref[...]
    for start in range(0, new_ref.shape[1], tile):
        span = pl.ds(start, tile)
        drive = partial_ref[:, span] + drives_ref[which, :, span] + dot(rates, kept_ref[pl.ds(rest, depth), span])
        new = updated(potential_ref[:, span], leak_ref[:, span], drive)
        new_ref[:, span] = new
        new_rates_ref[:, span] = jnp.tanh(new).astype(BF16)
    if pick:
        latest = picked(new_rates_ref, select_ref)
        block_ref[...] = packed([early_ref[...], middle_ref[...], latest])


def last_kernel(
    other_rates_ref, kept_ref, partial_ref, drives_ref, potential_ref, leak_ref, new_ref, scratch, sems, *, tile, which
):
    depth = other_rates_ref.shape[1]
    rest = kept_ref.shape[0] - depth
    rates = other_rates_ref[...]
    copies = []
    for n, start in enumerate(range(0, new_ref.shape[1], tile)):
        span = pl.ds(start, tile)
        drive = partial_ref[:, span] + drives_ref[which, :, span] + dot(rates, kept_ref[pl.ds(rest, depth), span])
        scratch[:, span] = updated(potential_ref[:, span], leak_ref[:, span], drive)
        copies.append(pltpu.make_async_copy(scratch.at[:, span], new_ref.at[:, span], sems.at[n]))
        copies[-1].start()
    for copy in copies:
        copy.wait()


def call(kernel, outs, in_specs, scratch=(), out_specs=None, estimate=None, **static):
    many = isinstance(outs, tuple)
    return pl.pallas_call(
        functools.partial(kernel, **static) if static else kernel,
        out_shape=outs,
        in_specs=in_specs,
        out_specs=out_specs or (tuple(VMEM_SPEC for _ in outs) if many else VMEM_SPEC),
        scratch_shapes=list(scratch),
        compiler_params=PARAMS,
        cost_estimate=estimate and pl.CostEstimate(flops=estimate, bytes_accessed=0, transcendentals=0),
        name=kernel.__name__,
    )


COST_OWN = 5_000_000_000
COST_OTHER = None
DRIVE_TILE = 1024
LEAST = 256


def local(
    proj_index, delays, past_rates, potential, stimulus, leak_rate, recurrence, ff_weight, fb_weight
):
    weight = remote(recurrence[0])
    stimulus, leak = resident(stimulus[0]), resident(leak_rate)
    forward, backward = resident(ff_weight[0]), resident(fb_weight[0])
    trials, columns = potential.shape[1:]
    chosen = proj_index.shape[1]
    depth = columns
    used = past_rates.shape[1] - 1
    sizes = [depth // 2] * 2 + parts(depth)
    chunks = tuple((sum(sizes[:n]), size) for n, size in enumerate(sizes))
    tile = largest_tile(columns, 1024)
    small = largest_tile(columns, 512)
    wide = pltpu.VMEM((trials, columns), F32)
    narrow = pltpu.VMEM((trials, columns), BF16)
    pick = pltpu.VMEM((trials, chosen), BF16)
    copies = pltpu.SemaphoreType.DMA

    def around(value):
        return resident(swapped(value, "area", 0)), resident(swapped(value, "area", 1))

    x, rates, block = call(
        first_kernel, (wide, narrow, pltpu.VMEM((trials, used * chosen), BF16)), [ANY_SPEC] * 2,
        [pltpu.VMEM((used, trials, chosen), BF16), copies((2,))],
    )(remote(potential[0]), remote(past_rates[0]))
    other_rates = resident(swapped(rates, "row", 0))
    past = around(block)[::-1]
    kept, partial, select, early = call(
        load_kernel, (pltpu.VMEM(weight.shape, BF16), wide, pltpu.VMEM((depth, chosen), BF16), pick),
        [VMEM_SPEC] * 2 + [ANY_SPEC] * 2, [pltpu.VMEM((1, chosen), jnp.int32), copies((len(chunks) + 1,))],
        chunks=chunks, tile=tile,
    )(resident(rates), other_rates, remote(proj_index), weight)
    kept, select = resident(kept), resident(select)
    maps = (forward, backward)

    def mapping(partial, x, start, *blocks):
        return call(
            maps_kernel, (wide, narrow, pltpu.VMEM((SUB - 1, trials, columns), F32)),
            [SMEM_SPEC] + [VMEM_SPEC] * (6 + len(blocks)), tile=DRIVE_TILE or columns, start=start,
        )(delays, resident(partial), resident(x), leak, stimulus, *maps, *blocks)

    x, rates, drives = mapping(partial, x, 0, *past)
    which = 0
    for instant in range(1, SLOTS):
        other_rates = resident(swapped(rates, "row", 0))
        own = (resident(rates), kept)
        if instant == 1:
            partial, middle = call(
                own_kernel, (wide, pick), [VMEM_SPEC] * 3, tile=tile, pick=True, estimate=COST_OWN,
            )(*own, select)
        else:
            partial = call(own_kernel, wide, [VMEM_SPEC] * 2, tile=tile, pick=False, estimate=COST_OWN)(*own)
        partial = resident(partial)
        if instant == SUB:
            partial = call(sum_kernel, wide, [VMEM_SPEC] * 3, tile=tile, estimate=COST_OWN)(other_rates, kept, partial)
            x, rates, drives = mapping(partial, x, SUB, *past, *recent)
            which = 0
            continue
        arguments = (other_rates, kept, partial, resident(drives), resident(x), leak)
        if instant + 1 == SLOTS:
            return call(
                last_kernel, jax.ShapeDtypeStruct((trials, columns), F32), [VMEM_SPEC] * 6,
                [pltpu.VMEM((trials, columns), F32), copies((columns // tile,))], ANY_SPEC, tile=tile, which=which,
            )(*arguments)[None]
        if instant + 1 == SUB - 1:
            x, rates, recent = call(
                other_kernel, (wide, narrow, pltpu.VMEM((trials, SUB * chosen), BF16)), [VMEM_SPEC] * 9,
                tile=small, which=which, pick=True, estimate=COST_OTHER,
            )(*arguments, select, resident(early), resident(middle))
            recent = around(recent)
        else:
            x, rates = call(
                other_kernel, (wide, narrow), [VMEM_SPEC] * 6, tile=small, which=which, pick=False, estimate=COST_OTHER,
            )(*arguments)
        which += 1


def solution(mesh):
    return jax.shard_map(
        local,
        mesh=mesh,
        in_specs=(
            P("area", "row"),
            P("area", None),
            P("area", None, "groups", "row"),
            P("area", "groups", "row"),
            P("area", "groups", "row"),
            P("area", "row"),
            P("area", None, "row"),
            P("area", None, "row"),
            P("area", None, "row"),
        ),
        out_specs=P("area", "groups", "row"),
        check_vma=False,
    )
```

```python
import functools

import jax
import jax.numpy as jnp
from jax import lax
from jax.experimental import pallas as pl
from jax.experimental.pallas import tpu as pltpu
from jax.sharding import PartitionSpec as P

SUB = 3
OUTER = 2
SLOTS = OUTER * SUB
BF16 = jnp.bfloat16
F32 = jnp.float32
VMEM_SPEC = pl.BlockSpec(memory_space=pltpu.VMEM)
SMEM_SPEC = pl.BlockSpec(memory_space=pltpu.SMEM)
ANY_SPEC = pl.BlockSpec(memory_space=pl.ANY)
PARAMS = pltpu.CompilerParams(vmem_limit_bytes=8 * 1024 * 1024)


def resident(value):
    return pltpu.with_memory_space_constraint(value, pltpu.VMEM)


def remote(value):
    return pltpu.with_memory_space_constraint(value, pltpu.HBM)


def swapped(value, axis, parity):
    count = lax.axis_size(axis)
    pairs = [(source, (source + (1 if source % 2 == parity else -1)) % count) for source in range(count)]
    return lax.ppermute(value, axis, pairs)


def largest_tile(size, most):
    return most if size % most == 0 else size


def parts(size):
    return [size // 2] + parts(size // 2) if size % 512 == 0 and size > LEAST else [size]


def shares(chosen):
    left = chosen % 128
    return chosen // 128, left, 128 // left if left and 128 % left == 0 else 1


def block_rows(used, trials, chosen):
    whole, left, group = shares(chosen)
    return used * whole * trials + (used // group * trials + used % group * trials // group if left else 0)


def packed(slots):
    used, (trials, chosen) = len(slots), slots[0].shape
    whole, left, group = shares(chosen)
    pieces = [slot[:, 128 * n:128 * n + 128] for slot in slots for n in range(whole)]
    if left:
        ends = [slot[:, 128 * whole:] for slot in slots]
        if left * group < 128:
            ends = [jnp.concatenate([end, jnp.zeros((trials, 128 - left), end.dtype)], axis=1) for end in ends]
        even = used // group * group
        few = trials // group
        pieces += [jnp.concatenate(ends[n:n + group], axis=1) for n in range(0, even, group)]
        pieces += [
            jnp.concatenate([end[n * few:(n + 1) * few] for n in range(group)], axis=1) for end in ends[even:]
        ]
    return jnp.concatenate(pieces, axis=0)


def unpacked(block, n, used, trials, chosen):
    whole, left, group = shares(chosen)
    pieces = [block[row * trials:(row + 1) * trials] for row in range(n * whole, (n + 1) * whole)]
    if left:
        start, even, few = used * whole * trials, used // group * group, trials // group
        if n < even:
            at = start + n // group * trials
            pieces.append(block[at:at + trials, n % group * left:(n % group + 1) * left])
        else:
            at = start + even // group * trials + (n - even) * few
            pieces.append(
                jnp.concatenate([block[at:at + few, m * left:(m + 1) * left] for m in range(group)], axis=0)
            )
    return pieces


def dot(a, b):
    rows = a.shape[0]
    if rows < 128:
        a = jnp.concatenate([a, jnp.zeros((128 - rows, a.shape[1]), a.dtype)], axis=0)
    return jnp.dot(a, b, preferred_element_type=F32)[:rows]


def picked(rates_ref, select_ref):
    return dot(rates_ref[...], select_ref[...]).astype(BF16)


def updated(potential, leak, drive):
    return potential + leak * (drive - potential)


def first_kernel(
    potential_ref, past_ref, kept_potential_ref, rates_ref, packed_ref, past_scratch, sems
):
    used = past_scratch.shape[0]
    trials = potential_ref.shape[0]
    halves = [pl.ds(start, trials // 2) for start in range(0, trials, trials // 2)]
    copies = [
        pltpu.make_async_copy(past_ref.at[pl.ds(past_ref.shape[0] - used, used)], past_scratch, sems.at[0])
    ] + [
        pltpu.make_async_copy(potential_ref.at[rows], kept_potential_ref.at[rows], sems.at[n + 1])
        for n, rows in enumerate(halves)
    ]
    for copy in copies:
        copy.start()
    copies[0].wait()
    packed_ref[...] = packed([past_scratch[n] for n in range(used)])
    for copy, rows in zip(copies[1:], halves):
        copy.wait()
        rates_ref[rows] = jnp.tanh(kept_potential_ref[rows]).astype(BF16)


def load_kernel(
    rates_ref, other_rates_ref, index_ref, weight_ref,
    kept_ref, partial_ref, select_ref, pick_ref, index_scratch, sems, *, chunks, tile
):
    depth = rates_ref.shape[1]
    block = lax.axis_index("row")
    own = pl.multiple_of(block * depth, depth)
    other = pl.multiple_of((1 - block) * depth, depth)
    index_copy = pltpu.make_async_copy(index_ref, index_scratch, sems.at[len(chunks)])
    index_copy.start()
    copies = []
    for n, (at, size) in enumerate(chunks):
        row = own + at if at < depth else other + at - depth
        copies.append(
            pltpu.make_async_copy(
                weight_ref.at[pl.ds(pl.multiple_of(row, 16), size)], kept_ref.at[pl.ds(at, size)], sems.at[n]
            )
        )
        copies[-1].start()
    columns = partial_ref.shape[1]
    for n, (at, size) in enumerate(chunks):
        if n == 1:
            index_copy.wait()
            rows = lax.broadcasted_iota(jnp.int32, select_ref.shape, 0)
            select_ref[...] = jnp.where(rows == index_scratch[...], 1.0, 0.0).astype(BF16)
            pick_ref[...] = picked(rates_ref, select_ref)
        copies[n].wait()
        left = rates_ref[:, pl.ds(at, size)] if at < depth else other_rates_ref[:, pl.ds(at - depth, size)]
        for start in range(0, columns, tile):
            span = pl.ds(start, tile)
            product = dot(left, kept_ref[pl.ds(at, size), span])
            partial_ref[:, span] = partial_ref[:, span] + product if n else product


def arrived(delay, instant, past, recent, trials, chosen):
    used = 2 * SUB - 1
    value = None
    for lag in range(SUB, 2 * SUB):
        place = instant - lag
        if place < 0:
            here = unpacked(past, used + place, used, trials, chosen)
        else:
            here = unpacked(recent, place, SUB, trials, chosen)
        value = here if value is None else [jnp.where(delay == lag, new, old) for new, old in zip(here, value)]
    return value


def mapped(delays_ref, instants, past_refs, recent_refs, forward_ref, backward_ref, stimulus_ref, tile):
    trials, columns = stimulus_ref.shape
    chosen = forward_ref.shape[0]
    odd = lax.axis_index("area") % 2 == 1
    sides = []
    for which in range(2):
        near = odd if which == 0 else jnp.logical_not(odd)
        past = jnp.where(near, past_refs[1][...], past_refs[0][...])
        recent = jnp.where(near, recent_refs[0][...], recent_refs[1][...]) if recent_refs else None
        delay = delays_ref[:, which:which + 1]
        values = [arrived(delay, n, past, recent, trials, chosen) for n in instants]
        sides.append([jnp.concatenate(piece, axis=0) for piece in zip(*values)])
    both = jnp.concatenate([piece for pair in zip(*sides) for piece in pair], axis=1)
    rows = [pl.ds(start, min(128, chosen - start)) for start in range(0, chosen, 128)]
    for start in range(0, columns, tile):
        span = pl.ds(start, tile)
        maps = jnp.concatenate([ref[part, span] for part in rows for ref in (forward_ref, backward_ref)], axis=0)
        drives = dot(both, maps)
        stimulus = stimulus_ref[:, span]
        yield span, [drives[n * trials:(n + 1) * trials] + stimulus for n in range(len(instants))]


def maps_kernel(delays_ref, partial_ref, potential_ref, leak_ref, stimulus_ref, forward_ref, backward_ref, *refs, tile, start):
    *blocks, new_ref, new_rates_ref, drives_ref = refs
    inputs = mapped(
        delays_ref, range(start, start + SUB), blocks[:2], blocks[2:], forward_ref, backward_ref, stimulus_ref, tile
    )
    for span, (drive, *later) in inputs:
        new = updated(potential_ref[:, span], leak_ref[:, span], partial_ref[:, span] + drive)
        new_ref[:, span] = new
        new_rates_ref[:, span] = jnp.tanh(new).astype(BF16)
        for n, drive in enumerate(later):
            drives_ref[n, :, span] = drive


def sum_kernel(other_rates_ref, kept_ref, partial_ref, whole_ref, *, tile):
    depth = other_rates_ref.shape[1]
    rest = kept_ref.shape[0] - depth
    for start in range(0, whole_ref.shape[1], tile):
        span = pl.ds(start, tile)
        whole_ref[:, span] = partial_ref[:, span] + dot(other_rates_ref[...], kept_ref[pl.ds(rest, depth), span])


def own_kernel(rates_ref, kept_ref, *refs, tile, pick):
    if pick:
        select_ref, partial_ref, pick_ref = refs
        pick_ref[...] = picked(rates_ref, select_ref)
    else:
        (partial_ref,) = refs
    depth = rates_ref.shape[1]
    for start in range(0, partial_ref.shape[1], tile):
        span = pl.ds(start, tile)
        partial_ref[:, span] = dot(rates_ref[...], kept_ref[pl.ds(0, depth), span])


def other_kernel(other_rates_ref, kept_ref, partial_ref, drives_ref, potential_ref, leak_ref, *refs, tile, which, pick):
    if pick:
        select_ref, early_ref, middle_ref, new_ref, new_rates_ref, block_ref = refs
    else:
        new_ref, new_rates_ref = refs
    depth = other_rates_ref.shape[1]
    rest = kept_ref.shape[0] - depth
    rates = other_rates_ref[...]
    for start in range(0, new_ref.shape[1], tile):
        span = pl.ds(start, tile)
        drive = partial_ref[:, span] + drives_ref[which, :, span] + dot(rates, kept_ref[pl.ds(rest, depth), span])
        new = updated(potential_ref[:, span], leak_ref[:, span], drive)
        new_ref[:, span] = new
        new_rates_ref[:, span] = jnp.tanh(new).astype(BF16)
    if pick:
        block_ref[...] = packed([early_ref[...], middle_ref[...], picked(new_rates_ref, select_ref)])


def last_kernel(
    other_rates_ref, kept_ref, partial_ref, drives_ref, potential_ref, leak_ref, new_ref, scratch, sems, *, tile, which
):
    depth = other_rates_ref.shape[1]
    rest = kept_ref.shape[0] - depth
    rates = other_rates_ref[...]
    copies = []
    for n, start in enumerate(range(0, new_ref.shape[1], tile)):
        span = pl.ds(start, tile)
        drive = partial_ref[:, span] + drives_ref[which, :, span] + dot(rates, kept_ref[pl.ds(rest, depth), span])
        scratch[:, span] = updated(potential_ref[:, span], leak_ref[:, span], drive)
        copies.append(pltpu.make_async_copy(scratch.at[:, span], new_ref.at[:, span], sems.at[n]))
        copies[-1].start()
    for copy in copies:
        copy.wait()


def call(kernel, outs, in_specs, scratch=(), out_specs=None, estimate=None, **static):
    many = isinstance(outs, tuple)
    return pl.pallas_call(
        functools.partial(kernel, **static) if static else kernel,
        out_shape=outs,
        in_specs=in_specs,
        out_specs=out_specs or (tuple(VMEM_SPEC for _ in outs) if many else VMEM_SPEC),
        scratch_shapes=list(scratch),
        compiler_params=PARAMS,
        cost_estimate=estimate and pl.CostEstimate(flops=estimate, bytes_accessed=0, transcendentals=0),
        name=kernel.__name__,
    )


COST_OWN = 5_000_000_000
COST_OTHER = None
DRIVE_TILE = 1024
LEAST = 256


def local(
    proj_index, delays, past_rates, potential, stimulus, leak_rate, recurrence, ff_weight, fb_weight
):
    weight = remote(recurrence[0])
    stimulus, leak = resident(stimulus[0]), resident(leak_rate)
    forward, backward = resident(ff_weight[0]), resident(fb_weight[0])
    trials, columns = potential.shape[1:]
    chosen = proj_index.shape[1]
    depth = columns
    used = past_rates.shape[1] - 1
    sizes = [depth // 2] * 2 + parts(depth)
    chunks = tuple((sum(sizes[:n]), size) for n, size in enumerate(sizes))
    tile = largest_tile(columns, 1024)
    small = largest_tile(columns, 512)
    wide = pltpu.VMEM((trials, columns), F32)
    narrow = pltpu.VMEM((trials, columns), BF16)
    pick = pltpu.VMEM((trials, chosen), BF16)
    copies = pltpu.SemaphoreType.DMA

    def around(value):
        return resident(swapped(value, "area", 0)), resident(swapped(value, "area", 1))

    x, rates, block = call(
        first_kernel, (wide, narrow, pltpu.VMEM((block_rows(used, trials, chosen), 128), BF16)), [ANY_SPEC] * 2,
        [pltpu.VMEM((used, trials, chosen), BF16), copies((3,))],
    )(remote(potential[0]), remote(past_rates[0]))
    other_rates = resident(swapped(rates, "row", 0))
    past = around(block)[::-1]
    kept, partial, select, early = call(
        load_kernel, (pltpu.VMEM(weight.shape, BF16), wide, pltpu.VMEM((depth, chosen), BF16), pick),
        [VMEM_SPEC] * 2 + [ANY_SPEC] * 2, [pltpu.VMEM((1, chosen), jnp.int32), copies((len(chunks) + 1,))],
        chunks=chunks, tile=tile,
    )(resident(rates), other_rates, remote(proj_index), weight)
    kept, select = resident(kept), resident(select)
    maps = (forward, backward)

    def mapping(partial, x, start, *blocks):
        return call(
            maps_kernel, (wide, narrow, pltpu.VMEM((SUB - 1, trials, columns), F32)),
            [VMEM_SPEC] * (7 + len(blocks)), tile=DRIVE_TILE or columns, start=start,
        )(resident(delays), resident(partial), resident(x), leak, stimulus, *maps, *blocks)

    x, rates, drives = mapping(partial, x, 0, *past)
    which = 0
    for instant in range(1, SLOTS):
        other_rates = resident(swapped(rates, "row", 0))
        own = (resident(rates), kept)
        if instant == 1:
            partial, middle = call(
                own_kernel, (wide, pick), [VMEM_SPEC] * 3, tile=tile, pick=True, estimate=COST_OWN,
            )(*own, select)
        else:
            partial = call(own_kernel, wide, [VMEM_SPEC] * 2, tile=tile, pick=False, estimate=COST_OWN)(*own)
        partial = resident(partial)
        if instant == SUB:
            partial = call(sum_kernel, wide, [VMEM_SPEC] * 3, tile=tile, estimate=COST_OWN)(other_rates, kept, partial)
            x, rates, drives = mapping(partial, x, SUB, *past, *recent)
            which = 0
            continue
        arguments = (other_rates, kept, partial, resident(drives), resident(x), leak)
        if instant + 1 == SLOTS:
            return call(
                last_kernel, jax.ShapeDtypeStruct((trials, columns), F32), [VMEM_SPEC] * 6,
                [pltpu.VMEM((trials, columns), F32), copies((columns // tile,))], ANY_SPEC, tile=tile, which=which,
            )(*arguments)[None]
        if instant + 1 == SUB - 1:
            x, rates, recent = call(
                other_kernel, (wide, narrow, pltpu.VMEM((block_rows(SUB, trials, chosen), 128), BF16)), [VMEM_SPEC] * 9,
                tile=small, which=which, pick=True, estimate=COST_OTHER,
            )(*arguments, select, resident(early), resident(middle))
            recent = around(recent)
        else:
            x, rates = call(
                other_kernel, (wide, narrow), [VMEM_SPEC] * 6, tile=small, which=which, pick=False, estimate=COST_OTHER,
            )(*arguments)
        which += 1


def solution(mesh):
    return jax.shard_map(
        local,
        mesh=mesh,
        in_specs=(
            P("area", "row"),
            P("area", None),
            P("area", None, "groups", "row"),
            P("area", "groups", "row"),
            P("area", "groups", "row"),
            P("area", "row"),
            P("area", None, "row"),
            P("area", None, "row"),
            P("area", None, "row"),
        ),
        out_specs=P("area", "groups", "row"),
        check_vma=False,
    )
```

```python
import functools

import jax
import jax.numpy as jnp
from jax import lax
from jax.experimental import pallas as pl
from jax.experimental.pallas import tpu as pltpu
from jax.sharding import PartitionSpec as P

SUB = 3
OUTER = 2
SLOTS = OUTER * SUB
BF16 = jnp.bfloat16
F32 = jnp.float32
VMEM_SPEC = pl.BlockSpec(memory_space=pltpu.VMEM)
SMEM_SPEC = pl.BlockSpec(memory_space=pltpu.SMEM)
ANY_SPEC = pl.BlockSpec(memory_space=pl.ANY)
PARAMS = pltpu.CompilerParams(vmem_limit_bytes=8 * 1024 * 1024)


def resident(value):
    return pltpu.with_memory_space_constraint(value, pltpu.VMEM)


def remote(value):
    return pltpu.with_memory_space_constraint(value, pltpu.HBM)


def swapped(value, axis, parity):
    count = lax.axis_size(axis)
    pairs = [(source, (source + (1 if source % 2 == parity else -1)) % count) for source in range(count)]
    return lax.ppermute(value, axis, pairs)


def largest_tile(size, most):
    return most if size % most == 0 else size


def parts(size):
    return [size // 2] + parts(size // 2) if size % 512 == 0 and size > LEAST else [size]


def shares(chosen):
    left = chosen % 128
    return chosen // 128, left, 128 // left if left and 128 % left == 0 else 1


def block_rows(used, trials, chosen):
    whole, left, group = shares(chosen)
    return used * whole * trials + (used // group * trials + used % group * trials // group if left else 0)


def packed(slots):
    used, (trials, chosen) = len(slots), slots[0].shape
    whole, left, group = shares(chosen)
    pieces = [slot[:, 128 * n:128 * n + 128] for slot in slots for n in range(whole)]
    if left:
        ends = [slot[:, 128 * whole:] for slot in slots]
        if left * group < 128:
            ends = [jnp.concatenate([end, jnp.zeros((trials, 128 - left), end.dtype)], axis=1) for end in ends]
        even = used // group * group
        few = trials // group
        pieces += [jnp.concatenate(ends[n:n + group], axis=1) for n in range(0, even, group)]
        pieces += [
            jnp.concatenate([end[n * few:(n + 1) * few] for n in range(group)], axis=1) for end in ends[even:]
        ]
    return jnp.concatenate(pieces, axis=0)


def unpacked(block, n, used, trials, chosen):
    whole, left, group = shares(chosen)
    pieces = [block[row * trials:(row + 1) * trials] for row in range(n * whole, (n + 1) * whole)]
    if left:
        start, even, few = used * whole * trials, used // group * group, trials // group
        if n < even:
            at = start + n // group * trials
            pieces.append(block[at:at + trials, n % group * left:(n % group + 1) * left])
        else:
            at = start + even // group * trials + (n - even) * few
            pieces.append(
                jnp.concatenate([block[at:at + few, m * left:(m + 1) * left] for m in range(group)], axis=0)
            )
    return pieces


def dot(a, b):
    rows = a.shape[0]
    if rows < 128:
        a = jnp.concatenate([a, jnp.zeros((128 - rows, a.shape[1]), a.dtype)], axis=0)
    return jnp.dot(a, b, preferred_element_type=F32)[:rows]


def picked(rates_ref, select_ref):
    return dot(rates_ref[...], select_ref[...]).astype(BF16)


def updated(potential, leak, drive):
    return potential + leak * (drive - potential)


def first_kernel(
    potential_ref, past_ref, kept_potential_ref, rates_ref, packed_ref, past_scratch, sems
):
    used = past_scratch.shape[0]
    trials = potential_ref.shape[0]
    halves = [pl.ds(start, trials // 2) for start in range(0, trials, trials // 2)]
    copies = [
        pltpu.make_async_copy(past_ref.at[pl.ds(past_ref.shape[0] - used, used)], past_scratch, sems.at[0])
    ] + [
        pltpu.make_async_copy(potential_ref.at[rows], kept_potential_ref.at[rows], sems.at[n + 1])
        for n, rows in enumerate(halves)
    ]
    for copy in copies:
        copy.start()
    copies[0].wait()
    packed_ref[...] = packed([past_scratch[n] for n in range(used)])
    for copy, rows in zip(copies[1:], halves):
        copy.wait()
        rates_ref[rows] = jnp.tanh(kept_potential_ref[rows]).astype(BF16)


def block_of(depth, other):
    block = lax.axis_index("row")
    return pl.ds(pl.multiple_of((1 - block if other else block) * depth, depth), depth)


def pick_kernel(rates_ref, index_ref, select_ref, pick_ref):
    rows = lax.broadcasted_iota(jnp.int32, select_ref.shape, 0)
    select_ref[...] = jnp.where(rows == index_ref[...], 1.0, 0.0).astype(BF16)
    pick_ref[...] = picked(rates_ref, select_ref)


def both_kernel(rates_ref, other_rates_ref, kept_ref, pick_ref, partial_ref, *, tile):
    del pick_ref
    depth, columns = rates_ref.shape[1], partial_ref.shape[1]
    for start in range(0, columns, tile):
        span = pl.ds(start, tile)
        partial_ref[:, span] = (
            dot(rates_ref[...], kept_ref[block_of(depth, False), span])
            + dot(other_rates_ref[...], kept_ref[block_of(depth, True), span])
        )


def arrived(delay, instant, past, recent, trials, chosen):
    used = 2 * SUB - 1
    value = None
    for lag in range(SUB, 2 * SUB):
        place = instant - lag
        if place < 0:
            here = unpacked(past, used + place, used, trials, chosen)
        else:
            here = unpacked(recent, place, SUB, trials, chosen)
        value = here if value is None else [jnp.where(delay == lag, new, old) for new, old in zip(here, value)]
    return value


def mapped(delays_ref, instants, past_refs, recent_refs, forward_ref, backward_ref, stimulus_ref, tile):
    trials, columns = stimulus_ref.shape
    chosen = forward_ref.shape[0]
    odd = lax.axis_index("area") % 2 == 1
    sides = []
    for which in range(2):
        near = odd if which == 0 else jnp.logical_not(odd)
        past = jnp.where(near, past_refs[1][...], past_refs[0][...])
        recent = jnp.where(near, recent_refs[1][...], recent_refs[0][...]) if recent_refs else None
        delay = delays_ref[:, which:which + 1]
        values = [arrived(delay, n, past, recent, trials, chosen) for n in instants]
        sides.append([jnp.concatenate(piece, axis=0) for piece in zip(*values)])
    both = jnp.concatenate([piece for pair in zip(*sides) for piece in pair], axis=1)
    rows = [pl.ds(start, min(128, chosen - start)) for start in range(0, chosen, 128)]
    for start in range(0, columns, tile):
        span = pl.ds(start, tile)
        maps = jnp.concatenate([ref[part, span] for part in rows for ref in (forward_ref, backward_ref)], axis=0)
        drives = dot(both, maps)
        stimulus = stimulus_ref[:, span]
        yield span, [drives[n * trials:(n + 1) * trials] + stimulus for n in range(len(instants))]


def maps_kernel(delays_ref, partial_ref, potential_ref, leak_ref, stimulus_ref, forward_ref, backward_ref, *refs, tile, start):
    *blocks, new_ref, new_rates_ref, drives_ref = refs
    inputs = mapped(
        delays_ref, range(start, start + SUB), blocks[:2], blocks[2:], forward_ref, backward_ref, stimulus_ref, tile
    )
    for span, (drive, *later) in inputs:
        new = updated(potential_ref[:, span], leak_ref[:, span], partial_ref[:, span] + drive)
        new_ref[:, span] = new
        new_rates_ref[:, span] = jnp.tanh(new).astype(BF16)
        for n, drive in enumerate(later):
            drives_ref[n, :, span] = drive


def sum_kernel(other_rates_ref, kept_ref, partial_ref, whole_ref, *, tile):
    depth = other_rates_ref.shape[1]
    rest = kept_ref.shape[0] - depth
    for start in range(0, whole_ref.shape[1], tile):
        span = pl.ds(start, tile)
        whole_ref[:, span] = partial_ref[:, span] + dot(other_rates_ref[...], kept_ref[block_of(depth, True), span])


def own_kernel(rates_ref, kept_ref, *refs, tile, pick):
    if pick:
        select_ref, partial_ref, pick_ref = refs
        pick_ref[...] = picked(rates_ref, select_ref)
    else:
        (partial_ref,) = refs
    own_product(rates_ref, kept_ref, partial_ref, tile)


def own_product(rates_ref, kept_ref, partial_ref, tile):
    depth = rates_ref.shape[1]
    for start in range(0, partial_ref.shape[1], tile):
        span = pl.ds(start, tile)
        partial_ref[:, span] = dot(rates_ref[...], kept_ref[block_of(depth, False), span])


def is_last():
    return lax.axis_index("area") >= lax.axis_size("area") - 2


def ahead_kernel(block_ref, rates_ref, kept_ref, same_block_ref, partial_ref, *, tile):
    same_block_ref[...] = block_ref[...]

    @pl.when(jnp.logical_not(is_last()))
    def _():
        own_product(rates_ref, kept_ref, partial_ref, tile)


def behind_kernel(partial_ref, rates_ref, kept_ref, whole_ref, *, tile):
    del partial_ref

    @pl.when(is_last())
    def _():
        own_product(rates_ref, kept_ref, whole_ref, tile)


def other_kernel(other_rates_ref, kept_ref, partial_ref, drives_ref, potential_ref, leak_ref, *refs, tile, which, pick):
    if pick:
        select_ref, early_ref, middle_ref, new_ref, new_rates_ref, block_ref = refs
    else:
        new_ref, new_rates_ref = refs
    depth = other_rates_ref.shape[1]
    rest = kept_ref.shape[0] - depth
    rates = other_rates_ref[...]
    for start in range(0, new_ref.shape[1], tile):
        span = pl.ds(start, tile)
        drive = partial_ref[:, span] + drives_ref[which, :, span] + dot(rates, kept_ref[block_of(depth, True), span])
        new = updated(potential_ref[:, span], leak_ref[:, span], drive)
        new_ref[:, span] = new
        new_rates_ref[:, span] = jnp.tanh(new).astype(BF16)
    if pick:
        block_ref[...] = packed([early_ref[...], middle_ref[...], picked(new_rates_ref, select_ref)])


def last_kernel(
    other_rates_ref, kept_ref, partial_ref, drives_ref, potential_ref, leak_ref, new_ref, scratch, sems, *, tile, which
):
    depth = other_rates_ref.shape[1]
    rest = kept_ref.shape[0] - depth
    rates = other_rates_ref[...]
    copies = []
    for n, start in enumerate(range(0, new_ref.shape[1], tile)):
        span = pl.ds(start, tile)
        drive = partial_ref[:, span] + drives_ref[which, :, span] + dot(rates, kept_ref[block_of(depth, True), span])
        scratch[:, span] = updated(potential_ref[:, span], leak_ref[:, span], drive)
        copies.append(pltpu.make_async_copy(scratch.at[:, span], new_ref.at[:, span], sems.at[n]))
        copies[-1].start()
    for copy in copies:
        copy.wait()


def call(kernel, outs, in_specs, scratch=(), out_specs=None, estimate=None, aliases=None, **static):
    many = isinstance(outs, tuple)
    return pl.pallas_call(
        functools.partial(kernel, **static) if static else kernel,
        out_shape=outs,
        in_specs=in_specs,
        out_specs=out_specs or (tuple(VMEM_SPEC for _ in outs) if many else VMEM_SPEC),
        scratch_shapes=list(scratch),
        input_output_aliases=aliases or {},
        compiler_params=PARAMS,
        cost_estimate=estimate and pl.CostEstimate(flops=estimate, bytes_accessed=0, transcendentals=0),
        name=kernel.__name__,
    )


COST_OWN = 5_000_000_000
COST_OTHER = None
FIRST_COST = 40_000_000_000
DRIVE_TILE = 1024
LEAST = 256


def local(
    proj_index, delays, past_rates, potential, stimulus, leak_rate, recurrence, ff_weight, fb_weight
):
    kept = resident(recurrence[0])
    stimulus, leak = resident(stimulus[0]), resident(leak_rate)
    forward, backward = resident(ff_weight[0]), resident(fb_weight[0])
    trials, columns = potential.shape[1:]
    chosen = proj_index.shape[1]
    depth = columns
    used = past_rates.shape[1] - 1
    sizes = [depth // 2] * 2 + parts(depth)
    chunks = tuple((sum(sizes[:n]), size) for n, size in enumerate(sizes))
    tile = largest_tile(columns, 1024)
    small = largest_tile(columns, 512)
    wide = pltpu.VMEM((trials, columns), F32)
    narrow = pltpu.VMEM((trials, columns), BF16)
    pick = pltpu.VMEM((trials, chosen), BF16)
    copies = pltpu.SemaphoreType.DMA

    def around(value):
        return resident(swapped(value, "area", 0)), resident(swapped(value, "area", 1))

    x, rates, block = call(
        first_kernel, (wide, narrow, pltpu.VMEM((block_rows(used, trials, chosen), 128), BF16)), [ANY_SPEC] * 2,
        [pltpu.VMEM((used, trials, chosen), BF16), copies((3,))], estimate=FIRST_COST,
    )(remote(potential[0]), remote(past_rates[0]))
    other_rates = resident(swapped(rates, "row", 0))
    past = around(block)[::-1]
    select, early = call(pick_kernel, (pltpu.VMEM((depth, chosen), BF16), pick), [VMEM_SPEC] * 2)(
        resident(rates), resident(proj_index)
    )
    select = resident(select)
    partial = call(both_kernel, wide, [VMEM_SPEC] * 4, tile=tile)(resident(rates), other_rates, kept, resident(early))
    maps = (forward, backward)

    def mapping(partial, x, start, *blocks):
        return call(
            maps_kernel, (wide, narrow, pltpu.VMEM((SUB - 1, trials, columns), F32)),
            [VMEM_SPEC] * (7 + len(blocks)), tile=DRIVE_TILE or columns, start=start,
        )(resident(delays), resident(partial), resident(x), leak, stimulus, *maps, *blocks)

    x, rates, drives = mapping(partial, x, 0, *past)
    which = 0
    for instant in range(1, SLOTS):
        other_rates = resident(swapped(rates, "row", 0))
        own = (resident(rates), kept)
        if instant == 1:
            partial, middle = call(
                own_kernel, (wide, pick), [VMEM_SPEC] * 3, tile=tile, pick=True, estimate=COST_OWN,
            )(*own, select)
        elif instant > SUB - 1:
            partial = call(own_kernel, wide, [VMEM_SPEC] * 2, tile=tile, pick=False, estimate=COST_OWN)(*own)
        partial = resident(partial)
        if instant == SUB:
            partial = call(sum_kernel, wide, [VMEM_SPEC] * 3, tile=tile, estimate=COST_OWN)(other_rates, kept, partial)
            x, rates, drives = mapping(partial, x, SUB, *past, *recent)
            which = 0
            continue
        arguments = (other_rates, kept, partial, resident(drives), resident(x), leak)
        if instant + 1 == SLOTS:
            return call(
                last_kernel, jax.ShapeDtypeStruct((trials, columns), F32), [VMEM_SPEC] * 6,
                [pltpu.VMEM((trials, columns), F32), copies((columns // tile,))], ANY_SPEC, tile=tile, which=which,
            )(*arguments)[None]
        if instant + 1 == SUB - 1:
            x, rates, recent = call(
                other_kernel, (wide, narrow, pltpu.VMEM((block_rows(SUB, trials, chosen), 128), BF16)), [VMEM_SPEC] * 9,
                tile=small, which=which, pick=True, estimate=COST_OTHER,
            )(*arguments, select, resident(early), resident(middle))
            recent, partial = call(
                ahead_kernel, (pltpu.VMEM(recent.shape, BF16), wide), [VMEM_SPEC] * 3, tile=tile, estimate=COST_OWN
            )(resident(recent), resident(rates), kept)
            recent = around(recent)[::-1]
            partial = call(behind_kernel, wide, [VMEM_SPEC] * 3, tile=tile, aliases={0: 0})(
                resident(partial), resident(rates), kept
            )
        else:
            x, rates = call(
                other_kernel, (wide, narrow), [VMEM_SPEC] * 6, tile=small, which=which, pick=False, estimate=COST_OTHER,
            )(*arguments)
        which += 1


def solution(mesh):
    return jax.shard_map(
        local,
        mesh=mesh,
        in_specs=(
            P("area", "row"),
            P("area", None),
            P("area", None, "groups", "row"),
            P("area", "groups", "row"),
            P("area", "groups", "row"),
            P("area", "row"),
            P("area", None, "row"),
            P("area", None, "row"),
            P("area", None, "row"),
        ),
        out_specs=P("area", "groups", "row"),
        check_vma=False,
    )
```

```python
import functools

import jax
import jax.numpy as jnp
from jax import lax
from jax.experimental import pallas as pl
from jax.experimental.pallas import tpu as pltpu
from jax.sharding import PartitionSpec as P

SUB = 3
OUTER = 2
SLOTS = OUTER * SUB
BF16 = jnp.bfloat16
F32 = jnp.float32
VMEM_SPEC = pl.BlockSpec(memory_space=pltpu.VMEM)
SMEM_SPEC = pl.BlockSpec(memory_space=pltpu.SMEM)
ANY_SPEC = pl.BlockSpec(memory_space=pl.ANY)
PARAMS = pltpu.CompilerParams(vmem_limit_bytes=8 * 1024 * 1024)


def resident(value):
    return pltpu.with_memory_space_constraint(value, pltpu.VMEM)


def remote(value):
    return pltpu.with_memory_space_constraint(value, pltpu.HBM)


def swapped(value, axis, parity):
    count = lax.axis_size(axis)
    pairs = [(source, (source + (1 if source % 2 == parity else -1)) % count) for source in range(count)]
    return lax.ppermute(value, axis, pairs)


def largest_tile(size, most):
    return most if size % most == 0 else size


def parts(size):
    return [size // 2] + parts(size // 2) if size % 512 == 0 and size > LEAST else [size]


def shares(chosen):
    left = chosen % 128
    return chosen // 128, left, 128 // left if left and 128 % left == 0 else 1


def block_rows(used, trials, chosen):
    whole, left, group = shares(chosen)
    return used * whole * trials + (used // group * trials + used % group * trials // group if left else 0)


def packed(slots):
    used, (trials, chosen) = len(slots), slots[0].shape
    whole, left, group = shares(chosen)
    pieces = [slot[:, 128 * n:128 * n + 128] for slot in slots for n in range(whole)]
    if left:
        ends = [slot[:, 128 * whole:] for slot in slots]
        if left * group < 128:
            ends = [jnp.concatenate([end, jnp.zeros((trials, 128 - left), end.dtype)], axis=1) for end in ends]
        even = used // group * group
        few = trials // group
        pieces += [jnp.concatenate(ends[n:n + group], axis=1) for n in range(0, even, group)]
        pieces += [
            jnp.concatenate([end[n * few:(n + 1) * few] for n in range(group)], axis=1) for end in ends[even:]
        ]
    return jnp.concatenate(pieces, axis=0)


def unpacked(block, n, used, trials, chosen):
    whole, left, group = shares(chosen)
    pieces = [block[row * trials:(row + 1) * trials] for row in range(n * whole, (n + 1) * whole)]
    if left:
        start, even, few = used * whole * trials, used // group * group, trials // group
        if n < even:
            at = start + n // group * trials
            pieces.append(block[at:at + trials, n % group * left:(n % group + 1) * left])
        else:
            at = start + even // group * trials + (n - even) * few
            pieces.append(
                jnp.concatenate([block[at:at + few, m * left:(m + 1) * left] for m in range(group)], axis=0)
            )
    return pieces


def dot(a, b):
    rows = a.shape[0]
    if rows < 128:
        a = jnp.concatenate([a, jnp.zeros((128 - rows, a.shape[1]), a.dtype)], axis=0)
    return jnp.dot(a, b, preferred_element_type=F32)[:rows]


def picked(rates_ref, select_ref):
    return dot(rates_ref[...], select_ref[...]).astype(BF16)


def updated(potential, leak, drive):
    return potential + leak * (drive - potential)


def first_kernel(
    potential_ref, past_ref, kept_potential_ref, rates_ref, packed_ref, past_scratch, sems
):
    used = past_scratch.shape[0]
    trials = potential_ref.shape[0]
    halves = [pl.ds(start, trials // 2) for start in range(0, trials, trials // 2)]
    copies = [
        pltpu.make_async_copy(past_ref.at[pl.ds(past_ref.shape[0] - used, used)], past_scratch, sems.at[0])
    ] + [
        pltpu.make_async_copy(potential_ref.at[rows], kept_potential_ref.at[rows], sems.at[n + 1])
        for n, rows in enumerate(halves)
    ]
    for copy in copies:
        copy.start()
    copies[0].wait()
    packed_ref[...] = packed([past_scratch[n] for n in range(used)])
    for copy, rows in zip(copies[1:], halves):
        copy.wait()
        rates_ref[rows] = jnp.tanh(kept_potential_ref[rows]).astype(BF16)


def block_of(depth, other):
    block = lax.axis_index("row")
    return pl.ds(pl.multiple_of((1 - block if other else block) * depth, depth), depth)


def pick_kernel(rates_ref, index_ref, select_ref, pick_ref):
    rows = lax.broadcasted_iota(jnp.int32, select_ref.shape, 0)
    select_ref[...] = jnp.where(rows == index_ref[...], 1.0, 0.0).astype(BF16)
    pick_ref[...] = picked(rates_ref, select_ref)


def both_kernel(rates_ref, other_rates_ref, kept_ref, pick_ref, partial_ref, *, tile):
    del pick_ref
    depth, columns = rates_ref.shape[1], partial_ref.shape[1]
    for start in range(0, columns, tile):
        span = pl.ds(start, tile)
        partial_ref[:, span] = (
            dot(rates_ref[...], kept_ref[block_of(depth, False), span])
            + dot(other_rates_ref[...], kept_ref[block_of(depth, True), span])
        )


def arrived(delay, instant, past, recent, trials, chosen):
    used = 2 * SUB - 1
    value = None
    for lag in range(SUB, 2 * SUB):
        place = instant - lag
        if place < 0:
            here = unpacked(past, used + place, used, trials, chosen)
        else:
            here = unpacked(recent, place, SUB, trials, chosen)
        value = here if value is None else [jnp.where(delay == lag, new, old) for new, old in zip(here, value)]
    return value


def mapped(delays_ref, instants, past_refs, recent_refs, forward_ref, backward_ref, stimulus_ref, tile):
    trials, columns = stimulus_ref.shape
    chosen = forward_ref.shape[0]
    odd = lax.axis_index("area") % 2 == 1
    sides = []
    for which in range(2):
        near = odd if which == 0 else jnp.logical_not(odd)
        past = jnp.where(near, past_refs[1][...], past_refs[0][...])
        recent = jnp.where(near, recent_refs[1][...], recent_refs[0][...]) if recent_refs else None
        delay = delays_ref[:, which:which + 1]
        values = [arrived(delay, n, past, recent, trials, chosen) for n in instants]
        sides.append([jnp.concatenate(piece, axis=0) for piece in zip(*values)])
    both = jnp.concatenate([piece for pair in zip(*sides) for piece in pair], axis=1)
    rows = [pl.ds(start, min(128, chosen - start)) for start in range(0, chosen, 128)]
    for start in range(0, columns, tile):
        span = pl.ds(start, tile)
        maps = jnp.concatenate([ref[part, span] for part in rows for ref in (forward_ref, backward_ref)], axis=0)
        drives = dot(both, maps)
        stimulus = stimulus_ref[:, span]
        yield span, [drives[n * trials:(n + 1) * trials] + stimulus for n in range(len(instants))]


def maps_kernel(
    delays_ref, partial_ref, potential_ref, leak_ref, stimulus_ref, forward_ref, backward_ref, *refs, tile, instants
):
    *blocks, new_ref, new_rates_ref, drives_ref = refs
    inputs = mapped(
        delays_ref, instants, blocks[:2], blocks[2:], forward_ref, backward_ref, stimulus_ref, tile
    )
    for span, (drive, *later) in inputs:
        new = updated(potential_ref[:, span], leak_ref[:, span], partial_ref[:, span] + drive)
        new_ref[:, span] = new
        new_rates_ref[:, span] = jnp.tanh(new).astype(BF16)
        for n, drive in enumerate(later):
            drives_ref[n, :, span] = drive


def sum_kernel(other_rates_ref, kept_ref, partial_ref, whole_ref, *, tile):
    depth = other_rates_ref.shape[1]
    rest = kept_ref.shape[0] - depth
    for start in range(0, whole_ref.shape[1], tile):
        span = pl.ds(start, tile)
        whole_ref[:, span] = partial_ref[:, span] + dot(other_rates_ref[...], kept_ref[block_of(depth, True), span])


def own_kernel(rates_ref, kept_ref, partial_ref, *, tile):
    own_product(rates_ref, kept_ref, partial_ref, tile)


def own_product(rates_ref, kept_ref, partial_ref, tile):
    depth = rates_ref.shape[1]
    for start in range(0, partial_ref.shape[1], tile):
        span = pl.ds(start, tile)
        partial_ref[:, span] = dot(rates_ref[...], kept_ref[block_of(depth, False), span])


def is_last():
    return lax.axis_index("area") >= lax.axis_size("area") - 2


def ahead_kernel(block_ref, rates_ref, kept_ref, same_block_ref, partial_ref, *, tile):
    same_block_ref[...] = block_ref[...]

    @pl.when(jnp.logical_not(is_last()))
    def _():
        own_product(rates_ref, kept_ref, partial_ref, tile)


def behind_kernel(
    partial_ref, rates_ref, kept_ref, delays_ref, stimulus_ref, forward_ref, backward_ref, *refs, tile, instant
):
    del partial_ref
    *blocks, whole_ref = refs

    @pl.when(is_last())
    def _():
        own_product(rates_ref, kept_ref, whole_ref, tile)

    inputs = mapped(delays_ref, (instant,), blocks, (), forward_ref, backward_ref, stimulus_ref, tile)
    for span, (drive,) in inputs:
        whole_ref[:, span] = whole_ref[:, span] + drive


def other_kernel(other_rates_ref, kept_ref, partial_ref, potential_ref, leak_ref, *refs, tile, which, pick):
    if which is not None:
        drives_ref, *refs = refs
    if pick:
        select_ref, early_ref, before_ref, new_ref, new_rates_ref, block_ref = refs
    else:
        new_ref, new_rates_ref = refs
    depth = other_rates_ref.shape[1]
    rest = kept_ref.shape[0] - depth
    rates = other_rates_ref[...]
    for start in range(0, new_ref.shape[1], tile):
        span = pl.ds(start, tile)
        drive = partial_ref[:, span] + dot(rates, kept_ref[block_of(depth, True), span])
        if which is not None:
            drive += drives_ref[which, :, span]
        new = updated(potential_ref[:, span], leak_ref[:, span], drive)
        new_ref[:, span] = new
        new_rates_ref[:, span] = jnp.tanh(new).astype(BF16)
    if pick:
        trials = early_ref.shape[0]
        both = dot(jnp.concatenate([before_ref[...], new_rates_ref[...]], axis=0), select_ref[...]).astype(BF16)
        block_ref[...] = packed([early_ref[...], both[:trials], both[trials:]])


def last_kernel(
    other_rates_ref, kept_ref, partial_ref, potential_ref, leak_ref, drives_ref, new_ref, scratch, sems, *, tile, which
):
    depth = other_rates_ref.shape[1]
    rest = kept_ref.shape[0] - depth
    rates = other_rates_ref[...]
    copies = []
    for n, start in enumerate(range(0, new_ref.shape[1], tile)):
        span = pl.ds(start, tile)
        drive = partial_ref[:, span] + drives_ref[which, :, span] + dot(rates, kept_ref[block_of(depth, True), span])
        scratch[:, span] = updated(potential_ref[:, span], leak_ref[:, span], drive)
        copies.append(pltpu.make_async_copy(scratch.at[:, span], new_ref.at[:, span], sems.at[n]))
        copies[-1].start()
    for copy in copies:
        copy.wait()


def call(kernel, outs, in_specs, scratch=(), out_specs=None, estimate=None, aliases=None, **static):
    many = isinstance(outs, tuple)
    return pl.pallas_call(
        functools.partial(kernel, **static) if static else kernel,
        out_shape=outs,
        in_specs=in_specs,
        out_specs=out_specs or (tuple(VMEM_SPEC for _ in outs) if many else VMEM_SPEC),
        scratch_shapes=list(scratch),
        input_output_aliases=aliases or {},
        compiler_params=PARAMS,
        cost_estimate=estimate and pl.CostEstimate(flops=estimate, bytes_accessed=0, transcendentals=0),
        name=kernel.__name__,
    )


COST_OWN = 5_000_000_000
COST_OTHER = None
FIRST_COST = 40_000_000_000
LEAST = 256


def local(
    proj_index, delays, past_rates, potential, stimulus, leak_rate, recurrence, ff_weight, fb_weight
):
    kept = resident(recurrence[0])
    stimulus, leak = resident(stimulus[0]), resident(leak_rate)
    forward, backward = resident(ff_weight[0]), resident(fb_weight[0])
    trials, columns = potential.shape[1:]
    chosen = proj_index.shape[1]
    depth = columns
    used = past_rates.shape[1] - 1
    sizes = [depth // 2] * 2 + parts(depth)
    chunks = tuple((sum(sizes[:n]), size) for n, size in enumerate(sizes))
    tile = largest_tile(columns, 1024)
    small = largest_tile(columns, 512)
    wide = pltpu.VMEM((trials, columns), F32)
    narrow = pltpu.VMEM((trials, columns), BF16)
    pick = pltpu.VMEM((trials, chosen), BF16)
    copies = pltpu.SemaphoreType.DMA

    def around(value):
        return resident(swapped(value, "area", 0)), resident(swapped(value, "area", 1))

    x, rates, block = call(
        first_kernel, (wide, narrow, pltpu.VMEM((block_rows(used, trials, chosen), 128), BF16)), [ANY_SPEC] * 2,
        [pltpu.VMEM((used, trials, chosen), BF16), copies((3,))], estimate=FIRST_COST,
    )(remote(potential[0]), remote(past_rates[0]))
    other_rates = resident(swapped(rates, "row", 0))
    past = around(block)[::-1]
    select, early = call(pick_kernel, (pltpu.VMEM((depth, chosen), BF16), pick), [VMEM_SPEC] * 2)(
        resident(rates), resident(proj_index)
    )
    select = resident(select)
    partial = call(both_kernel, wide, [VMEM_SPEC] * 4, tile=tile)(resident(rates), other_rates, kept, resident(early))
    maps = (forward, backward)

    def mapping(partial, x, instants, *blocks):
        return call(
            maps_kernel, (wide, narrow, pltpu.VMEM((len(instants) - 1, trials, columns), F32)),
            [VMEM_SPEC] * (7 + len(blocks)), tile=tile, instants=instants,
        )(resident(delays), resident(partial), resident(x), leak, stimulus, *maps, *blocks)

    x, rates, drives = mapping(partial, x, tuple(range(SUB - 1)), *past)
    which = 0
    for instant in range(1, SLOTS):
        other_rates = resident(swapped(rates, "row", 0))
        if instant != SUB - 1:
            partial = call(own_kernel, wide, [VMEM_SPEC] * 2, tile=tile, estimate=COST_OWN)(resident(rates), kept)
        partial = resident(partial)
        if instant == SUB:
            partial = call(sum_kernel, wide, [VMEM_SPEC] * 3, tile=tile, estimate=COST_OWN)(other_rates, kept, partial)
            x, rates, drives = mapping(partial, x, tuple(range(SUB, SLOTS)), *past, *recent)
            which = 0
            continue
        arguments = (other_rates, kept, partial, resident(x), leak)
        if instant == SUB - 1:
            x, rates = call(
                other_kernel, (wide, narrow), [VMEM_SPEC] * 5, tile=small, which=None, pick=False, estimate=COST_OTHER,
            )(*arguments)
            continue
        arguments += (resident(drives),)
        if instant + 1 == SLOTS:
            return call(
                last_kernel, jax.ShapeDtypeStruct((trials, columns), F32), [VMEM_SPEC] * 6,
                [pltpu.VMEM((trials, columns), F32), copies((columns // tile,))], ANY_SPEC, tile=tile, which=which,
            )(*arguments)[None]
        if instant + 1 == SUB - 1:
            before = resident(rates)
            x, rates, recent = call(
                other_kernel, (wide, narrow, pltpu.VMEM((block_rows(SUB, trials, chosen), 128), BF16)), [VMEM_SPEC] * 9,
                tile=small, which=which, pick=True, estimate=COST_OTHER,
            )(*arguments, select, resident(early), before)
            recent, partial = call(
                ahead_kernel, (pltpu.VMEM(recent.shape, BF16), wide), [VMEM_SPEC] * 3, tile=tile, estimate=COST_OWN
            )(resident(recent), resident(rates), kept)
            recent = around(recent)[::-1]
            partial = call(behind_kernel, wide, [VMEM_SPEC] * 9, tile=tile, aliases={0: 0}, instant=instant + 1)(
                resident(partial), resident(rates), kept, resident(delays), stimulus, *maps, *past
            )
        else:
            x, rates = call(
                other_kernel, (wide, narrow), [VMEM_SPEC] * 6, tile=small, which=which, pick=False, estimate=COST_OTHER,
            )(*arguments)
        which += 1


def solution(mesh):
    return jax.shard_map(
        local,
        mesh=mesh,
        in_specs=(
            P("area", "row"),
            P("area", None),
            P("area", None, "groups", "row"),
            P("area", "groups", "row"),
            P("area", "groups", "row"),
            P("area", "row"),
            P("area", None, "row"),
            P("area", None, "row"),
            P("area", None, "row"),
        ),
        out_specs=P("area", "groups", "row"),
        check_vma=False,
    )
```

```python
import functools

import jax
import jax.numpy as jnp
from jax import lax
from jax.experimental import pallas as pl
from jax.experimental.pallas import tpu as pltpu
from jax.sharding import PartitionSpec as P

SUB = 3
OUTER = 2
SLOTS = OUTER * SUB
BF16 = jnp.bfloat16
F32 = jnp.float32
VMEM_SPEC = pl.BlockSpec(memory_space=pltpu.VMEM)
SMEM_SPEC = pl.BlockSpec(memory_space=pltpu.SMEM)
ANY_SPEC = pl.BlockSpec(memory_space=pl.ANY)
PARAMS = pltpu.CompilerParams(vmem_limit_bytes=8 * 1024 * 1024)


def resident(value):
    return pltpu.with_memory_space_constraint(value, pltpu.VMEM)


def remote(value):
    return pltpu.with_memory_space_constraint(value, pltpu.HBM)


def swapped(value, axis, parity):
    count = lax.axis_size(axis)
    pairs = [(source, (source + (1 if source % 2 == parity else -1)) % count) for source in range(count)]
    return lax.ppermute(value, axis, pairs)


def largest_tile(size, most):
    return most if size % most == 0 else size


def parts(size):
    return [size // 2] + parts(size // 2) if size % 512 == 0 and size > LEAST else [size]


def shares(chosen):
    left = chosen % 128
    return chosen // 128, left, 128 // left if left and 128 % left == 0 else 1


def block_rows(used, trials, chosen):
    whole, left, group = shares(chosen)
    return used * whole * trials + (used // group * trials + used % group * trials // group if left else 0)


def packed(slots):
    used, (trials, chosen) = len(slots), slots[0].shape
    whole, left, group = shares(chosen)
    pieces = [slot[:, 128 * n:128 * n + 128] for slot in slots for n in range(whole)]
    if left:
        ends = [slot[:, 128 * whole:] for slot in slots]
        if left * group < 128:
            ends = [jnp.concatenate([end, jnp.zeros((trials, 128 - left), end.dtype)], axis=1) for end in ends]
        even = used // group * group
        few = trials // group
        pieces += [jnp.concatenate(ends[n:n + group], axis=1) for n in range(0, even, group)]
        pieces += [
            jnp.concatenate([end[n * few:(n + 1) * few] for n in range(group)], axis=1) for end in ends[even:]
        ]
    return jnp.concatenate(pieces, axis=0)


def unpacked(block, n, used, trials, chosen):
    whole, left, group = shares(chosen)
    pieces = [block[row * trials:(row + 1) * trials] for row in range(n * whole, (n + 1) * whole)]
    if left:
        start, even, few = used * whole * trials, used // group * group, trials // group
        if n < even:
            at = start + n // group * trials
            pieces.append(block[at:at + trials, n % group * left:(n % group + 1) * left])
        else:
            at = start + even // group * trials + (n - even) * few
            pieces.append(
                jnp.concatenate([block[at:at + few, m * left:(m + 1) * left] for m in range(group)], axis=0)
            )
    return pieces


def dot(a, b):
    rows = a.shape[0]
    if rows < 128:
        a = jnp.concatenate([a, jnp.zeros((128 - rows, a.shape[1]), a.dtype)], axis=0)
    return jnp.dot(a, b, preferred_element_type=F32)[:rows]


def picked(rates_ref, select_ref):
    return dot(rates_ref[...], select_ref[...]).astype(BF16)


def updated(potential, leak, drive):
    return potential + leak * (drive - potential)


def pack_kernel(past_ref, packed_ref, past_scratch, sems):
    used = past_scratch.shape[0]
    copy = pltpu.make_async_copy(past_ref.at[pl.ds(past_ref.shape[0] - used, used)], past_scratch, sems.at[0])
    copy.start()
    copy.wait()
    packed_ref[...] = packed([past_scratch[n] for n in range(used)])


def rates_kernel(block_ref, potential_ref, kept_potential_ref, rates_ref, sems):
    del block_ref
    copy = pltpu.make_async_copy(potential_ref, kept_potential_ref, sems.at[0])
    copy.start()
    copy.wait()
    rates_ref[...] = jnp.tanh(kept_potential_ref[...]).astype(BF16)


def block_of(depth, other):
    block = lax.axis_index("row")
    return pl.ds(pl.multiple_of((1 - block if other else block) * depth, depth), depth)


def pick_kernel(rates_ref, index_ref, select_ref, pick_ref):
    rows = lax.broadcasted_iota(jnp.int32, select_ref.shape, 0)
    select_ref[...] = jnp.where(rows == index_ref[...], 1.0, 0.0).astype(BF16)
    pick_ref[...] = picked(rates_ref, select_ref)


def after_pick_kernel(rates_ref, kept_ref, pick_ref, partial_ref, *, tile):
    del pick_ref
    own_product(rates_ref, kept_ref, partial_ref, tile)


def arrived(delay, instant, past, recent, trials, chosen):
    used = 2 * SUB - 1
    value = None
    for lag in range(SUB, 2 * SUB):
        place = instant - lag
        if place < 0:
            here = unpacked(past, used + place, used, trials, chosen)
        else:
            here = unpacked(recent, place, SUB, trials, chosen)
        value = here if value is None else [jnp.where(delay == lag, new, old) for new, old in zip(here, value)]
    return value


def mapped(delays_ref, instants, past_refs, recent_refs, forward_ref, backward_ref, stimulus_ref, tile):
    trials, columns = stimulus_ref.shape
    chosen = forward_ref.shape[0]
    odd = lax.axis_index("area") % 2 == 1
    sides = []
    for which in range(2):
        near = odd if which == 0 else jnp.logical_not(odd)
        past = jnp.where(near, past_refs[1][...], past_refs[0][...])
        recent = jnp.where(near, recent_refs[1][...], recent_refs[0][...]) if recent_refs else None
        delay = delays_ref[:, which:which + 1]
        values = [arrived(delay, n, past, recent, trials, chosen) for n in instants]
        sides.append([jnp.concatenate(piece, axis=0) for piece in zip(*values)])
    both = jnp.concatenate([piece for pair in zip(*sides) for piece in pair], axis=1)
    rows = [pl.ds(start, min(128, chosen - start)) for start in range(0, chosen, 128)]
    for start in range(0, columns, tile):
        span = pl.ds(start, tile)
        maps = jnp.concatenate([ref[part, span] for part in rows for ref in (forward_ref, backward_ref)], axis=0)
        drives = dot(both, maps)
        stimulus = stimulus_ref[:, span]
        yield span, [drives[n * trials:(n + 1) * trials] + stimulus for n in range(len(instants))]


def maps_kernel(
    delays_ref, partial_ref, potential_ref, leak_ref, stimulus_ref, forward_ref, backward_ref, *refs, tile, instants
):
    *blocks, new_ref, new_rates_ref, drives_ref = refs
    inputs = mapped(
        delays_ref, instants, blocks[:2], blocks[2:], forward_ref, backward_ref, stimulus_ref, tile
    )
    for span, (drive, *later) in inputs:
        new = updated(potential_ref[:, span], leak_ref[:, span], partial_ref[:, span] + drive)
        new_ref[:, span] = new
        new_rates_ref[:, span] = jnp.tanh(new).astype(BF16)
        for n, drive in enumerate(later):
            drives_ref[n, :, span] = drive


def sum_kernel(other_rates_ref, kept_ref, partial_ref, whole_ref, *, tile):
    depth = other_rates_ref.shape[1]
    rest = kept_ref.shape[0] - depth
    for start in range(0, whole_ref.shape[1], tile):
        span = pl.ds(start, tile)
        whole_ref[:, span] = partial_ref[:, span] + dot(other_rates_ref[...], kept_ref[block_of(depth, True), span])


def own_kernel(rates_ref, kept_ref, partial_ref, *, tile):
    own_product(rates_ref, kept_ref, partial_ref, tile)


def own_product(rates_ref, kept_ref, partial_ref, tile):
    depth = rates_ref.shape[1]
    for start in range(0, partial_ref.shape[1], tile):
        span = pl.ds(start, tile)
        partial_ref[:, span] = dot(rates_ref[...], kept_ref[block_of(depth, False), span])


def is_last():
    return lax.axis_index("area") >= lax.axis_size("area") - 2


def ahead_kernel(block_ref, rates_ref, kept_ref, same_block_ref, partial_ref, *, tile):
    same_block_ref[...] = block_ref[...]

    @pl.when(jnp.logical_not(is_last()))
    def _():
        own_product(rates_ref, kept_ref, partial_ref, tile)


def behind_kernel(
    partial_ref, rates_ref, kept_ref, delays_ref, stimulus_ref, forward_ref, backward_ref, *refs, tile, instant
):
    del partial_ref
    *blocks, whole_ref = refs

    @pl.when(is_last())
    def _():
        own_product(rates_ref, kept_ref, whole_ref, tile)

    inputs = mapped(delays_ref, (instant,), blocks, (), forward_ref, backward_ref, stimulus_ref, tile)
    for span, (drive,) in inputs:
        whole_ref[:, span] = whole_ref[:, span] + drive


def other_kernel(other_rates_ref, kept_ref, partial_ref, potential_ref, leak_ref, *refs, tile, which, pick):
    if which is not None:
        drives_ref, *refs = refs
    if pick:
        select_ref, early_ref, before_ref, new_ref, new_rates_ref, block_ref = refs
    else:
        new_ref, new_rates_ref = refs
    depth = other_rates_ref.shape[1]
    rest = kept_ref.shape[0] - depth
    rates = other_rates_ref[...]
    for start in range(0, new_ref.shape[1], tile):
        span = pl.ds(start, tile)
        drive = partial_ref[:, span] + dot(rates, kept_ref[block_of(depth, True), span])
        if which is not None:
            drive += drives_ref[which, :, span]
        new = updated(potential_ref[:, span], leak_ref[:, span], drive)
        new_ref[:, span] = new
        new_rates_ref[:, span] = jnp.tanh(new).astype(BF16)
    if pick:
        trials = early_ref.shape[0]
        both = dot(jnp.concatenate([before_ref[...], new_rates_ref[...]], axis=0), select_ref[...]).astype(BF16)
        block_ref[...] = packed([early_ref[...], both[:trials], both[trials:]])


def last_kernel(
    other_rates_ref, kept_ref, partial_ref, potential_ref, leak_ref, drives_ref, new_ref, scratch, sems, *, tile, which
):
    depth = other_rates_ref.shape[1]
    rest = kept_ref.shape[0] - depth
    rates = other_rates_ref[...]
    copies = []
    for n, start in enumerate(range(0, new_ref.shape[1], tile)):
        span = pl.ds(start, tile)
        drive = partial_ref[:, span] + drives_ref[which, :, span] + dot(rates, kept_ref[block_of(depth, True), span])
        scratch[:, span] = updated(potential_ref[:, span], leak_ref[:, span], drive)
        copies.append(pltpu.make_async_copy(scratch.at[:, span], new_ref.at[:, span], sems.at[n]))
        copies[-1].start()
    for copy in copies:
        copy.wait()


def call(kernel, outs, in_specs, scratch=(), out_specs=None, estimate=None, aliases=None, **static):
    many = isinstance(outs, tuple)
    return pl.pallas_call(
        functools.partial(kernel, **static) if static else kernel,
        out_shape=outs,
        in_specs=in_specs,
        out_specs=out_specs or (tuple(VMEM_SPEC for _ in outs) if many else VMEM_SPEC),
        scratch_shapes=list(scratch),
        input_output_aliases=aliases or {},
        compiler_params=PARAMS,
        cost_estimate=estimate and pl.CostEstimate(flops=estimate, bytes_accessed=0, transcendentals=0),
        name=kernel.__name__,
    )


COST_OWN = 5_000_000_000
COST_OTHER = None
RATES_COST = None
PICK_COST = 5000000000
FIRST_COST = 40_000_000_000
LEAST = 256


def local(
    proj_index, delays, past_rates, potential, stimulus, leak_rate, recurrence, ff_weight, fb_weight
):
    kept = resident(recurrence[0])
    stimulus, leak = resident(stimulus[0]), resident(leak_rate)
    forward, backward = resident(ff_weight[0]), resident(fb_weight[0])
    trials, columns = potential.shape[1:]
    chosen = proj_index.shape[1]
    depth = columns
    used = past_rates.shape[1] - 1
    sizes = [depth // 2] * 2 + parts(depth)
    chunks = tuple((sum(sizes[:n]), size) for n, size in enumerate(sizes))
    tile = largest_tile(columns, 1024)
    small = largest_tile(columns, 512)
    wide = pltpu.VMEM((trials, columns), F32)
    narrow = pltpu.VMEM((trials, columns), BF16)
    pick = pltpu.VMEM((trials, chosen), BF16)
    copies = pltpu.SemaphoreType.DMA

    def around(value):
        return resident(swapped(value, "area", 0)), resident(swapped(value, "area", 1))

    block = call(
        pack_kernel, pltpu.VMEM((block_rows(used, trials, chosen), 128), BF16), [ANY_SPEC],
        [pltpu.VMEM((used, trials, chosen), BF16), copies((1,))], estimate=FIRST_COST,
    )(remote(past_rates[0]))
    x, rates = call(rates_kernel, (wide, narrow), [VMEM_SPEC, ANY_SPEC], [copies((1,))], estimate=RATES_COST)(
        resident(block), remote(potential[0])
    )
    other_rates = resident(swapped(rates, "row", 0))
    past = around(block)[::-1]
    select, early = call(pick_kernel, (pltpu.VMEM((depth, chosen), BF16), pick), [VMEM_SPEC] * 2, estimate=PICK_COST)(
        resident(rates), resident(proj_index)
    )
    select = resident(select)
    partial = call(after_pick_kernel, wide, [VMEM_SPEC] * 3, tile=tile, estimate=COST_OWN)(
        resident(rates), kept, resident(early)
    )
    partial = call(sum_kernel, wide, [VMEM_SPEC] * 3, tile=tile)(other_rates, kept, resident(partial))
    maps = (forward, backward)

    def mapping(partial, x, instants, *blocks):
        return call(
            maps_kernel, (wide, narrow, pltpu.VMEM((len(instants) - 1, trials, columns), F32)),
            [VMEM_SPEC] * (7 + len(blocks)), tile=tile, instants=instants,
        )(resident(delays), resident(partial), resident(x), leak, stimulus, *maps, *blocks)

    x, rates, drives = mapping(partial, x, tuple(range(SUB - 1)), *past)
    which = 0
    for instant in range(1, SLOTS):
        other_rates = resident(swapped(rates, "row", 0))
        if instant != SUB - 1:
            partial = call(own_kernel, wide, [VMEM_SPEC] * 2, tile=tile, estimate=COST_OWN)(resident(rates), kept)
        partial = resident(partial)
        if instant == SUB:
            partial = call(sum_kernel, wide, [VMEM_SPEC] * 3, tile=tile, estimate=COST_OWN)(other_rates, kept, partial)
            x, rates, drives = mapping(partial, x, tuple(range(SUB, SLOTS)), *past, *recent)
            which = 0
            continue
        arguments = (other_rates, kept, partial, resident(x), leak)
        if instant == SUB - 1:
            x, rates = call(
                other_kernel, (wide, narrow), [VMEM_SPEC] * 5, tile=small, which=None, pick=False, estimate=COST_OTHER,
            )(*arguments)
            continue
        arguments += (resident(drives),)
        if instant + 1 == SLOTS:
            return call(
                last_kernel, jax.ShapeDtypeStruct((trials, columns), F32), [VMEM_SPEC] * 6,
                [pltpu.VMEM((trials, columns), F32), copies((columns // tile,))], ANY_SPEC, tile=tile, which=which,
            )(*arguments)[None]
        if instant + 1 == SUB - 1:
            before = resident(rates)
            x, rates, recent = call(
                other_kernel, (wide, narrow, pltpu.VMEM((block_rows(SUB, trials, chosen), 128), BF16)), [VMEM_SPEC] * 9,
                tile=small, which=which, pick=True, estimate=COST_OTHER,
            )(*arguments, select, resident(early), before)
            recent, partial = call(
                ahead_kernel, (pltpu.VMEM(recent.shape, BF16), wide), [VMEM_SPEC] * 3, tile=tile, estimate=COST_OWN
            )(resident(recent), resident(rates), kept)
            recent = around(recent)[::-1]
            partial = call(behind_kernel, wide, [VMEM_SPEC] * 9, tile=tile, aliases={0: 0}, instant=instant + 1)(
                resident(partial), resident(rates), kept, resident(delays), stimulus, *maps, *past
            )
        else:
            x, rates = call(
                other_kernel, (wide, narrow), [VMEM_SPEC] * 6, tile=small, which=which, pick=False, estimate=COST_OTHER,
            )(*arguments)
        which += 1


def solution(mesh):
    return jax.shard_map(
        local,
        mesh=mesh,
        in_specs=(
            P("area", "row"),
            P("area", None),
            P("area", None, "groups", "row"),
            P("area", "groups", "row"),
            P("area", "groups", "row"),
            P("area", "row"),
            P("area", None, "row"),
            P("area", None, "row"),
            P("area", None, "row"),
        ),
        out_specs=P("area", "groups", "row"),
        check_vma=False,
    )
```

```python
import functools

import jax
import jax.numpy as jnp
from jax import lax
from jax.experimental import pallas as pl
from jax.experimental.pallas import tpu as pltpu
from jax.sharding import PartitionSpec as P

SUB = 3
OUTER = 2
SLOTS = OUTER * SUB
BF16 = jnp.bfloat16
F32 = jnp.float32
VMEM_SPEC = pl.BlockSpec(memory_space=pltpu.VMEM)
SMEM_SPEC = pl.BlockSpec(memory_space=pltpu.SMEM)
ANY_SPEC = pl.BlockSpec(memory_space=pl.ANY)
PARAMS = pltpu.CompilerParams(vmem_limit_bytes=8 * 1024 * 1024)


def resident(value):
    return pltpu.with_memory_space_constraint(value, pltpu.VMEM)


def remote(value):
    return pltpu.with_memory_space_constraint(value, pltpu.HBM)


def swapped(value, axis, parity):
    count = lax.axis_size(axis)
    pairs = [(source, (source + (1 if source % 2 == parity else -1)) % count) for source in range(count)]
    return lax.ppermute(value, axis, pairs)


def largest_tile(size, most):
    return most if size % most == 0 else size


def parts(size):
    return [size // 2] + parts(size // 2) if size % 512 == 0 and size > LEAST else [size]


def shares(chosen):
    left = chosen % 128
    return chosen // 128, left, 128 // left if left and 128 % left == 0 else 1


def block_rows(used, trials, chosen):
    whole, left, group = shares(chosen)
    return used * whole * trials + (used // group * trials + used % group * trials // group if left else 0)


def packed(slots):
    used, (trials, chosen) = len(slots), slots[0].shape
    whole, left, group = shares(chosen)
    pieces = [slot[:, 128 * n:128 * n + 128] for slot in slots for n in range(whole)]
    if left:
        ends = [slot[:, 128 * whole:] for slot in slots]
        if left * group < 128:
            ends = [jnp.concatenate([end, jnp.zeros((trials, 128 - left), end.dtype)], axis=1) for end in ends]
        even = used // group * group
        few = trials // group
        pieces += [jnp.concatenate(ends[n:n + group], axis=1) for n in range(0, even, group)]
        pieces += [
            jnp.concatenate([end[n * few:(n + 1) * few] for n in range(group)], axis=1) for end in ends[even:]
        ]
    return jnp.concatenate(pieces, axis=0)


def unpacked(block, n, used, trials, chosen):
    whole, left, group = shares(chosen)
    pieces = [block[row * trials:(row + 1) * trials] for row in range(n * whole, (n + 1) * whole)]
    if left:
        start, even, few = used * whole * trials, used // group * group, trials // group
        if n < even:
            at = start + n // group * trials
            pieces.append(block[at:at + trials, n % group * left:(n % group + 1) * left])
        else:
            at = start + even // group * trials + (n - even) * few
            pieces.append(
                jnp.concatenate([block[at:at + few, m * left:(m + 1) * left] for m in range(group)], axis=0)
            )
    return pieces


def dot(a, b):
    rows = a.shape[0]
    if rows < 128:
        a = jnp.concatenate([a, jnp.zeros((128 - rows, a.shape[1]), a.dtype)], axis=0)
    return jnp.dot(a, b, preferred_element_type=F32)[:rows]


def updated(potential, leak, drive):
    return potential + leak * (drive - potential)


def pack_kernel(past_ref, packed_ref, past_scratch, sems):
    used = past_scratch.shape[0]
    copy = pltpu.make_async_copy(past_ref.at[pl.ds(past_ref.shape[0] - used, used)], past_scratch, sems.at[0])
    copy.start()
    copy.wait()
    packed_ref[...] = packed([past_scratch[n] for n in range(used)])


def rates_kernel(block_ref, potential_ref, kept_potential_ref, rates_ref, sems):
    del block_ref
    copy = pltpu.make_async_copy(potential_ref, kept_potential_ref, sems.at[0])
    copy.start()
    copy.wait()
    rates_ref[...] = jnp.tanh(kept_potential_ref[...]).astype(BF16)


def block_of(depth, other):
    block = lax.axis_index("row")
    return pl.ds(pl.multiple_of((1 - block if other else block) * depth, depth), depth)


def select_kernel(rates_ref, index_ref, select_ref):
    del rates_ref
    rows = lax.broadcasted_iota(jnp.int32, select_ref.shape, 0)
    select_ref[...] = jnp.where(rows == index_ref[...], 1.0, 0.0).astype(BF16)


def after_pick_kernel(rates_ref, kept_ref, pick_ref, partial_ref, *, tile):
    del pick_ref
    own_product(rates_ref, kept_ref, partial_ref, tile)


def arrived(delay, instant, past, recent, trials, chosen):
    used = 2 * SUB - 1
    value = None
    for lag in range(SUB, 2 * SUB):
        place = instant - lag
        if place < 0:
            here = unpacked(past, used + place, used, trials, chosen)
        else:
            here = unpacked(recent, place, SUB, trials, chosen)
        value = here if value is None else [jnp.where(delay == lag, new, old) for new, old in zip(here, value)]
    return value


def mapped(delays_ref, instants, past_refs, recent_refs, forward_ref, backward_ref, stimulus_ref, tile):
    trials, columns = stimulus_ref.shape
    chosen = forward_ref.shape[0]
    odd = lax.axis_index("area") % 2 == 1
    sides = []
    for which in range(2):
        near = odd if which == 0 else jnp.logical_not(odd)
        past = jnp.where(near, past_refs[1][...], past_refs[0][...])
        recent = jnp.where(near, recent_refs[1][...], recent_refs[0][...]) if recent_refs else None
        delay = delays_ref[:, which:which + 1]
        values = [arrived(delay, n, past, recent, trials, chosen) for n in instants]
        sides.append([jnp.concatenate(piece, axis=0) for piece in zip(*values)])
    both = jnp.concatenate([piece for pair in zip(*sides) for piece in pair], axis=1)
    rows = [pl.ds(start, min(128, chosen - start)) for start in range(0, chosen, 128)]
    for start in range(0, columns, tile):
        span = pl.ds(start, tile)
        maps = jnp.concatenate([ref[part, span] for part in rows for ref in (forward_ref, backward_ref)], axis=0)
        drives = dot(both, maps)
        stimulus = stimulus_ref[:, span]
        yield span, [drives[n * trials:(n + 1) * trials] + stimulus for n in range(len(instants))]


def maps_kernel(
    delays_ref, partial_ref, potential_ref, leak_ref, stimulus_ref, forward_ref, backward_ref, *refs, tile, instants
):
    *blocks, new_ref, new_rates_ref, drives_ref = refs
    inputs = mapped(
        delays_ref, instants, blocks[:2], blocks[2:], forward_ref, backward_ref, stimulus_ref, tile
    )
    for span, (drive, *later) in inputs:
        new = updated(potential_ref[:, span], leak_ref[:, span], partial_ref[:, span] + drive)
        new_ref[:, span] = new
        new_rates_ref[:, span] = jnp.tanh(new).astype(BF16)
        for n, drive in enumerate(later):
            drives_ref[n, :, span] = drive


def sum_kernel(other_rates_ref, kept_ref, partial_ref, whole_ref, *, tile):
    depth = other_rates_ref.shape[1]
    rest = kept_ref.shape[0] - depth
    for start in range(0, whole_ref.shape[1], tile):
        span = pl.ds(start, tile)
        whole_ref[:, span] = partial_ref[:, span] + dot(other_rates_ref[...], kept_ref[block_of(depth, True), span])


def own_kernel(rates_ref, kept_ref, partial_ref, *, tile):
    own_product(rates_ref, kept_ref, partial_ref, tile)


def own_product(rates_ref, kept_ref, partial_ref, tile):
    depth = rates_ref.shape[1]
    for start in range(0, partial_ref.shape[1], tile):
        span = pl.ds(start, tile)
        partial_ref[:, span] = dot(rates_ref[...], kept_ref[block_of(depth, False), span])


def is_last():
    return lax.axis_index("area") >= lax.axis_size("area") - 2


def ahead_kernel(block_ref, rates_ref, kept_ref, same_block_ref, partial_ref, *, tile):
    same_block_ref[...] = block_ref[...]

    @pl.when(jnp.logical_not(is_last()))
    def _():
        own_product(rates_ref, kept_ref, partial_ref, tile)


def behind_kernel(
    partial_ref, rates_ref, kept_ref, delays_ref, stimulus_ref, forward_ref, backward_ref, *refs, tile, instant
):
    del partial_ref
    *blocks, whole_ref = refs

    @pl.when(is_last())
    def _():
        own_product(rates_ref, kept_ref, whole_ref, tile)

    inputs = mapped(delays_ref, (instant,), blocks, (), forward_ref, backward_ref, stimulus_ref, tile)
    for span, (drive,) in inputs:
        whole_ref[:, span] = whole_ref[:, span] + drive


def other_kernel(other_rates_ref, kept_ref, partial_ref, potential_ref, leak_ref, *refs, tile, which, pick):
    if which is not None:
        drives_ref, *refs = refs
    if pick:
        select_ref, first_ref, before_ref, new_ref, new_rates_ref, block_ref = refs
    else:
        new_ref, new_rates_ref = refs
    depth = other_rates_ref.shape[1]
    rest = kept_ref.shape[0] - depth
    rates = other_rates_ref[...]
    for start in range(0, new_ref.shape[1], tile):
        span = pl.ds(start, tile)
        drive = partial_ref[:, span] + dot(rates, kept_ref[block_of(depth, True), span])
        if which is not None:
            drive += drives_ref[which, :, span]
        new = updated(potential_ref[:, span], leak_ref[:, span], drive)
        new_ref[:, span] = new
        new_rates_ref[:, span] = jnp.tanh(new).astype(BF16)
    if pick:
        trials = first_ref.shape[0]
        every = jnp.concatenate([first_ref[...], before_ref[...], new_rates_ref[...]], axis=0)
        picks = dot(every, select_ref[...]).astype(BF16)
        block_ref[...] = packed([picks[n * trials:(n + 1) * trials] for n in range(SUB)])


def last_kernel(
    other_rates_ref, kept_ref, partial_ref, potential_ref, leak_ref, drives_ref, new_ref, scratch, sems, *, tile, which
):
    depth = other_rates_ref.shape[1]
    rest = kept_ref.shape[0] - depth
    rates = other_rates_ref[...]
    copies = []
    for n, start in enumerate(range(0, new_ref.shape[1], tile)):
        span = pl.ds(start, tile)
        drive = partial_ref[:, span] + drives_ref[which, :, span] + dot(rates, kept_ref[block_of(depth, True), span])
        scratch[:, span] = updated(potential_ref[:, span], leak_ref[:, span], drive)
        copies.append(pltpu.make_async_copy(scratch.at[:, span], new_ref.at[:, span], sems.at[n]))
        copies[-1].start()
    for copy in copies:
        copy.wait()


def call(kernel, outs, in_specs, scratch=(), out_specs=None, estimate=None, aliases=None, **static):
    many = isinstance(outs, tuple)
    return pl.pallas_call(
        functools.partial(kernel, **static) if static else kernel,
        out_shape=outs,
        in_specs=in_specs,
        out_specs=out_specs or (tuple(VMEM_SPEC for _ in outs) if many else VMEM_SPEC),
        scratch_shapes=list(scratch),
        input_output_aliases=aliases or {},
        compiler_params=PARAMS,
        cost_estimate=estimate and pl.CostEstimate(flops=estimate, bytes_accessed=0, transcendentals=0),
        name=kernel.__name__,
    )


COST_OWN = 5_000_000_000
COST_OTHER = None
RATES_COST = None
PICK_COST = 5000000000
FIRST_COST = 40_000_000_000
LEAST = 256


def local(
    proj_index, delays, past_rates, potential, stimulus, leak_rate, recurrence, ff_weight, fb_weight
):
    kept = resident(recurrence[0])
    stimulus, leak = resident(stimulus[0]), resident(leak_rate)
    forward, backward = resident(ff_weight[0]), resident(fb_weight[0])
    trials, columns = potential.shape[1:]
    chosen = proj_index.shape[1]
    depth = columns
    used = past_rates.shape[1] - 1
    sizes = [depth // 2] * 2 + parts(depth)
    chunks = tuple((sum(sizes[:n]), size) for n, size in enumerate(sizes))
    tile = largest_tile(columns, 1024)
    small = largest_tile(columns, 512)
    wide = pltpu.VMEM((trials, columns), F32)
    narrow = pltpu.VMEM((trials, columns), BF16)
    pick = pltpu.VMEM((trials, chosen), BF16)
    copies = pltpu.SemaphoreType.DMA

    def around(value):
        return resident(swapped(value, "area", 0)), resident(swapped(value, "area", 1))

    block = call(
        pack_kernel, pltpu.VMEM((block_rows(used, trials, chosen), 128), BF16), [ANY_SPEC],
        [pltpu.VMEM((used, trials, chosen), BF16), copies((1,))], estimate=FIRST_COST,
    )(remote(past_rates[0]))
    x, rates = call(rates_kernel, (wide, narrow), [VMEM_SPEC, ANY_SPEC], [copies((1,))], estimate=RATES_COST)(
        resident(block), remote(potential[0])
    )
    other_rates = resident(swapped(rates, "row", 0))
    past = around(block)[::-1]
    first_rates = resident(rates)
    select = resident(call(select_kernel, pltpu.VMEM((depth, chosen), BF16), [VMEM_SPEC] * 2, estimate=PICK_COST)(
        first_rates, resident(proj_index)
    ))
    partial = call(after_pick_kernel, wide, [VMEM_SPEC] * 3, tile=tile, estimate=COST_OWN)(
        first_rates, kept, select
    )
    partial = call(sum_kernel, wide, [VMEM_SPEC] * 3, tile=tile)(other_rates, kept, resident(partial))
    maps = (forward, backward)

    def mapping(partial, x, instants, *blocks):
        return call(
            maps_kernel, (wide, narrow, pltpu.VMEM((len(instants) - 1, trials, columns), F32)),
            [VMEM_SPEC] * (7 + len(blocks)), tile=tile, instants=instants,
        )(resident(delays), resident(partial), resident(x), leak, stimulus, *maps, *blocks)

    x, rates, drives = mapping(partial, x, tuple(range(SUB - 1)), *past)
    which = 0
    for instant in range(1, SLOTS):
        other_rates = resident(swapped(rates, "row", 0))
        if instant != SUB - 1:
            partial = call(own_kernel, wide, [VMEM_SPEC] * 2, tile=tile, estimate=COST_OWN)(resident(rates), kept)
        partial = resident(partial)
        if instant == SUB:
            partial = call(sum_kernel, wide, [VMEM_SPEC] * 3, tile=tile, estimate=COST_OWN)(other_rates, kept, partial)
            x, rates, drives = mapping(partial, x, tuple(range(SUB, SLOTS)), *past, *recent)
            which = 0
            continue
        arguments = (other_rates, kept, partial, resident(x), leak)
        if instant == SUB - 1:
            x, rates = call(
                other_kernel, (wide, narrow), [VMEM_SPEC] * 5, tile=small, which=None, pick=False, estimate=COST_OTHER,
            )(*arguments)
            continue
        arguments += (resident(drives),)
        if instant + 1 == SLOTS:
            return call(
                last_kernel, jax.ShapeDtypeStruct((trials, columns), F32), [VMEM_SPEC] * 6,
                [pltpu.VMEM((trials, columns), F32), copies((columns // tile,))], ANY_SPEC, tile=tile, which=which,
            )(*arguments)[None]
        if instant + 1 == SUB - 1:
            before = resident(rates)
            x, rates, recent = call(
                other_kernel, (wide, narrow, pltpu.VMEM((block_rows(SUB, trials, chosen), 128), BF16)), [VMEM_SPEC] * 9,
                tile=small, which=which, pick=True, estimate=COST_OTHER,
            )(*arguments, select, first_rates, before)
            recent, partial = call(
                ahead_kernel, (pltpu.VMEM(recent.shape, BF16), wide), [VMEM_SPEC] * 3, tile=tile, estimate=COST_OWN
            )(resident(recent), resident(rates), kept)
            recent = around(recent)[::-1]
            partial = call(behind_kernel, wide, [VMEM_SPEC] * 9, tile=tile, aliases={0: 0}, instant=instant + 1)(
                resident(partial), resident(rates), kept, resident(delays), stimulus, *maps, *past
            )
        else:
            x, rates = call(
                other_kernel, (wide, narrow), [VMEM_SPEC] * 6, tile=small, which=which, pick=False, estimate=COST_OTHER,
            )(*arguments)
        which += 1


def solution(mesh):
    return jax.shard_map(
        local,
        mesh=mesh,
        in_specs=(
            P("area", "row"),
            P("area", None),
            P("area", None, "groups", "row"),
            P("area", "groups", "row"),
            P("area", "groups", "row"),
            P("area", "row"),
            P("area", None, "row"),
            P("area", None, "row"),
            P("area", None, "row"),
        ),
        out_specs=P("area", "groups", "row"),
        check_vma=False,
    )
```

```python
import functools

import jax
import jax.numpy as jnp
from jax import lax
from jax.experimental import pallas as pl
from jax.experimental.pallas import tpu as pltpu
from jax.sharding import PartitionSpec as P

SUB = 3
OUTER = 2
SLOTS = OUTER * SUB
BF16 = jnp.bfloat16
F32 = jnp.float32
VMEM_SPEC = pl.BlockSpec(memory_space=pltpu.VMEM)
SMEM_SPEC = pl.BlockSpec(memory_space=pltpu.SMEM)
ANY_SPEC = pl.BlockSpec(memory_space=pl.ANY)
PARAMS = pltpu.CompilerParams(vmem_limit_bytes=8 * 1024 * 1024)


def resident(value):
    return pltpu.with_memory_space_constraint(value, pltpu.VMEM)


def remote(value):
    return pltpu.with_memory_space_constraint(value, pltpu.HBM)


def swapped(value, axis, parity):
    count = lax.axis_size(axis)
    pairs = [(source, (source + (1 if source % 2 == parity else -1)) % count) for source in range(count)]
    return lax.ppermute(value, axis, pairs)


def largest_tile(size, most):
    return most if size % most == 0 else size


def parts(size):
    return [size // 2] + parts(size // 2) if size % 512 == 0 and size > LEAST else [size]


def shares(chosen):
    left = chosen % 128
    return chosen // 128, left, 128 // left if left and 128 % left == 0 else 1


def block_rows(used, trials, chosen):
    whole, left, group = shares(chosen)
    return used * whole * trials + (used // group * trials + used % group * trials // group if left else 0)


def packed(slots):
    used, (trials, chosen) = len(slots), slots[0].shape
    whole, left, group = shares(chosen)
    pieces = [slot[:, 128 * n:128 * n + 128] for slot in slots for n in range(whole)]
    if left:
        ends = [slot[:, 128 * whole:] for slot in slots]
        if left * group < 128:
            ends = [jnp.concatenate([end, jnp.zeros((trials, 128 - left), end.dtype)], axis=1) for end in ends]
        even = used // group * group
        few = trials // group
        pieces += [jnp.concatenate(ends[n:n + group], axis=1) for n in range(0, even, group)]
        pieces += [
            jnp.concatenate([end[n * few:(n + 1) * few] for n in range(group)], axis=1) for end in ends[even:]
        ]
    return jnp.concatenate(pieces, axis=0)


def unpacked(block, n, used, trials, chosen):
    whole, left, group = shares(chosen)
    pieces = [block[row * trials:(row + 1) * trials] for row in range(n * whole, (n + 1) * whole)]
    if left:
        start, even, few = used * whole * trials, used // group * group, trials // group
        if n < even:
            at = start + n // group * trials
            pieces.append(block[at:at + trials, n % group * left:(n % group + 1) * left])
        else:
            at = start + even // group * trials + (n - even) * few
            pieces.append(
                jnp.concatenate([block[at:at + few, m * left:(m + 1) * left] for m in range(group)], axis=0)
            )
    return pieces


def dot(a, b):
    rows = a.shape[0]
    if rows < 128:
        a = jnp.concatenate([a, jnp.zeros((128 - rows, a.shape[1]), a.dtype)], axis=0)
    return jnp.dot(a, b, preferred_element_type=F32)[:rows]


def updated(potential, leak, drive):
    return potential + leak * (drive - potential)


def pack_kernel(past_ref, packed_ref, past_scratch, sems):
    used = past_scratch.shape[0]
    copy = pltpu.make_async_copy(past_ref.at[pl.ds(past_ref.shape[0] - used, used)], past_scratch, sems.at[0])
    copy.start()
    copy.wait()
    packed_ref[...] = packed([past_scratch[n] for n in range(used)])


def rates_kernel(block_ref, potential_ref, kept_potential_ref, rates_ref, sems):
    del block_ref
    copy = pltpu.make_async_copy(potential_ref, kept_potential_ref, sems.at[0])
    copy.start()
    copy.wait()
    rates_ref[...] = jnp.tanh(kept_potential_ref[...]).astype(BF16)


def block_of(depth, other):
    block = lax.axis_index("row")
    return pl.ds(pl.multiple_of((1 - block if other else block) * depth, depth), depth)


def select_kernel(rates_ref, index_ref, select_ref):
    del rates_ref
    rows = lax.broadcasted_iota(jnp.int32, select_ref.shape, 0)
    select_ref[...] = jnp.where(rows == index_ref[...], 1.0, 0.0).astype(BF16)


def after_pick_kernel(rates_ref, kept_ref, pick_ref, partial_ref, *, tile):
    del pick_ref
    own_product(rates_ref, kept_ref, partial_ref, tile)


def arrived(delay, instant, past, recent, trials, chosen):
    used = 2 * SUB - 1
    value = None
    for lag in range(SUB, 2 * SUB):
        place = instant - lag
        if place < 0:
            here = unpacked(past, used + place, used, trials, chosen)
        else:
            here = unpacked(recent, place, SUB, trials, chosen)
        value = here if value is None else [jnp.where(delay == lag, new, old) for new, old in zip(here, value)]
    return value


def mapped(delays_ref, instants, past_refs, recent_refs, forward_ref, backward_ref, stimulus_ref, tile):
    trials, columns = stimulus_ref.shape
    chosen = forward_ref.shape[0]
    odd = lax.axis_index("area") % 2 == 1
    sides = []
    for which in range(2):
        near = odd if which == 0 else jnp.logical_not(odd)
        past = jnp.where(near, past_refs[1][...], past_refs[0][...])
        recent = jnp.where(near, recent_refs[1][...], recent_refs[0][...]) if recent_refs else None
        delay = delays_ref[:, which:which + 1]
        values = [arrived(delay, n, past, recent, trials, chosen) for n in instants]
        sides.append([jnp.concatenate(piece, axis=0) for piece in zip(*values)])
    both = jnp.concatenate([piece for pair in zip(*sides) for piece in pair], axis=1)
    rows = [pl.ds(start, min(128, chosen - start)) for start in range(0, chosen, 128)]
    for start in range(0, columns, tile):
        span = pl.ds(start, tile)
        maps = jnp.concatenate([ref[part, span] for part in rows for ref in (forward_ref, backward_ref)], axis=0)
        drives = dot(both, maps)
        stimulus = stimulus_ref[:, span]
        yield span, [drives[n * trials:(n + 1) * trials] + stimulus for n in range(len(instants))]


def maps_kernel(
    delays_ref, partial_ref, potential_ref, leak_ref, stimulus_ref, forward_ref, backward_ref, *refs, tile, instants
):
    *blocks, new_ref, new_rates_ref, drives_ref = refs
    inputs = mapped(
        delays_ref, instants, blocks[:2], blocks[2:], forward_ref, backward_ref, stimulus_ref, tile
    )
    for span, (drive, *later) in inputs:
        new = updated(potential_ref[:, span], leak_ref[:, span], partial_ref[:, span] + drive)
        new_ref[:, span] = new
        new_rates_ref[:, span] = jnp.tanh(new).astype(BF16)
        for n, drive in enumerate(later):
            drives_ref[n, :, span] = drive


def sum_kernel(other_rates_ref, kept_ref, partial_ref, whole_ref, *, tile):
    depth = other_rates_ref.shape[1]
    rest = kept_ref.shape[0] - depth
    for start in range(0, whole_ref.shape[1], tile):
        span = pl.ds(start, tile)
        whole_ref[:, span] = partial_ref[:, span] + dot(other_rates_ref[...], kept_ref[block_of(depth, True), span])


def own_kernel(rates_ref, kept_ref, partial_ref, *, tile):
    own_product(rates_ref, kept_ref, partial_ref, tile)


def own_product(rates_ref, kept_ref, partial_ref, tile):
    depth = rates_ref.shape[1]
    for start in range(0, partial_ref.shape[1], tile):
        span = pl.ds(start, tile)
        partial_ref[:, span] = dot(rates_ref[...], kept_ref[block_of(depth, False), span])


def is_last():
    return lax.axis_index("area") >= lax.axis_size("area") - 2


def ahead_kernel(block_ref, rates_ref, kept_ref, same_block_ref, partial_ref, *, tile):
    same_block_ref[...] = block_ref[...]

    @pl.when(jnp.logical_not(is_last()))
    def _():
        own_product(rates_ref, kept_ref, partial_ref, tile)


def behind_kernel(
    partial_ref, rates_ref, kept_ref, delays_ref, stimulus_ref, forward_ref, backward_ref, *refs, tile, instant
):
    del partial_ref
    *blocks, whole_ref = refs

    @pl.when(is_last())
    def _():
        own_product(rates_ref, kept_ref, whole_ref, tile)

    inputs = mapped(delays_ref, (instant,), blocks, (), forward_ref, backward_ref, stimulus_ref, tile)
    for span, (drive,) in inputs:
        whole_ref[:, span] = whole_ref[:, span] + drive


def other_kernel(other_rates_ref, kept_ref, partial_ref, potential_ref, leak_ref, *refs, tile, which, pick):
    if which is not None:
        drives_ref, *refs = refs
    if pick:
        select_ref, first_ref, before_ref, new_ref, new_rates_ref, block_ref = refs
    else:
        new_ref, new_rates_ref = refs
    depth = other_rates_ref.shape[1]
    rest = kept_ref.shape[0] - depth
    rates = other_rates_ref[...]
    for start in range(0, new_ref.shape[1], tile):
        span = pl.ds(start, tile)
        drive = partial_ref[:, span] + dot(rates, kept_ref[block_of(depth, True), span])
        if which is not None:
            drive += drives_ref[which, :, span]
        new = updated(potential_ref[:, span], leak_ref[:, span], drive)
        new_ref[:, span] = new
        new_rates_ref[:, span] = jnp.tanh(new).astype(BF16)
    if pick:
        trials = first_ref.shape[0]
        every = jnp.concatenate([first_ref[...], before_ref[...], new_rates_ref[...]], axis=0)
        picks = dot(every, select_ref[...]).astype(BF16)
        block_ref[...] = packed([picks[n * trials:(n + 1) * trials] for n in range(SUB)])


def last_kernel(
    other_rates_ref, kept_ref, partial_ref, potential_ref, leak_ref, drives_ref, new_ref, scratch, sems, *, tile, which
):
    depth = other_rates_ref.shape[1]
    rest = kept_ref.shape[0] - depth
    rates = other_rates_ref[...]
    copies = []
    for n, start in enumerate(range(0, new_ref.shape[1], tile)):
        span = pl.ds(start, tile)
        drive = partial_ref[:, span] + drives_ref[which, :, span] + dot(rates, kept_ref[block_of(depth, True), span])
        scratch[:, span] = updated(potential_ref[:, span], leak_ref[:, span], drive)
        copies.append(pltpu.make_async_copy(scratch.at[:, span], new_ref.at[:, span], sems.at[n]))
        copies[-1].start()
    for copy in copies:
        copy.wait()


def call(kernel, outs, in_specs, scratch=(), out_specs=None, estimate=None, aliases=None, **static):
    many = isinstance(outs, tuple)
    return pl.pallas_call(
        functools.partial(kernel, **static) if static else kernel,
        out_shape=outs,
        in_specs=in_specs,
        out_specs=out_specs or (tuple(VMEM_SPEC for _ in outs) if many else VMEM_SPEC),
        scratch_shapes=list(scratch),
        input_output_aliases=aliases or {},
        compiler_params=PARAMS,
        cost_estimate=estimate and pl.CostEstimate(flops=estimate, bytes_accessed=0, transcendentals=0),
        name=kernel.__name__,
    )


COST_OWN = 5_000_000_000
COST_OTHER = None
RATES_COST = None
PICK_COST = 5000000000
FIRST_COST = 40_000_000_000
LEAST = 256


def local(
    proj_index, delays, past_rates, potential, stimulus, leak_rate, recurrence, ff_weight, fb_weight
):
    kept = resident(recurrence[0])
    stimulus, leak = resident(stimulus[0]), resident(leak_rate)
    forward, backward = resident(ff_weight[0]), resident(fb_weight[0])
    trials, columns = potential.shape[1:]
    chosen = proj_index.shape[1]
    depth = columns
    used = past_rates.shape[1] - 1
    sizes = [depth // 2] * 2 + parts(depth)
    chunks = tuple((sum(sizes[:n]), size) for n, size in enumerate(sizes))
    tile = largest_tile(columns, 2048)
    half = largest_tile(columns, 1024)
    small = largest_tile(columns, 2048)
    wide = pltpu.VMEM((trials, columns), F32)
    narrow = pltpu.VMEM((trials, columns), BF16)
    pick = pltpu.VMEM((trials, chosen), BF16)
    copies = pltpu.SemaphoreType.DMA

    def around(value):
        return resident(swapped(value, "area", 0)), resident(swapped(value, "area", 1))

    block = call(
        pack_kernel, pltpu.VMEM((block_rows(used, trials, chosen), 128), BF16), [ANY_SPEC],
        [pltpu.VMEM((used, trials, chosen), BF16), copies((1,))], estimate=FIRST_COST,
    )(remote(past_rates[0]))
    x, rates = call(rates_kernel, (wide, narrow), [VMEM_SPEC, ANY_SPEC], [copies((1,))], estimate=RATES_COST)(
        resident(block), remote(potential[0])
    )
    other_rates = resident(swapped(rates, "row", 0))
    past = around(block)[::-1]
    first_rates = resident(rates)
    select = resident(call(select_kernel, pltpu.VMEM((depth, chosen), BF16), [VMEM_SPEC] * 2, estimate=PICK_COST)(
        first_rates, resident(proj_index)
    ))
    partial = call(after_pick_kernel, wide, [VMEM_SPEC] * 3, tile=tile, estimate=COST_OWN)(
        first_rates, kept, select
    )
    partial = call(sum_kernel, wide, [VMEM_SPEC] * 3, tile=tile)(other_rates, kept, resident(partial))
    maps = (forward, backward)

    def mapping(partial, x, instants, *blocks):
        return call(
            maps_kernel, (wide, narrow, pltpu.VMEM((len(instants) - 1, trials, columns), F32)),
            [VMEM_SPEC] * (7 + len(blocks)), tile=tile, instants=instants,
        )(resident(delays), resident(partial), resident(x), leak, stimulus, *maps, *blocks)

    x, rates, drives = mapping(partial, x, tuple(range(SUB - 1)), *past)
    which = 0
    for instant in range(1, SLOTS):
        other_rates = resident(swapped(rates, "row", 0))
        if instant != SUB - 1:
            partial = call(own_kernel, wide, [VMEM_SPEC] * 2, tile=tile, estimate=COST_OWN)(resident(rates), kept)
        partial = resident(partial)
        if instant == SUB:
            partial = call(sum_kernel, wide, [VMEM_SPEC] * 3, tile=tile, estimate=COST_OWN)(other_rates, kept, partial)
            x, rates, drives = mapping(partial, x, tuple(range(SUB, SLOTS)), *past, *recent)
            which = 0
            continue
        arguments = (other_rates, kept, partial, resident(x), leak)
        if instant == SUB - 1:
            x, rates = call(
                other_kernel, (wide, narrow), [VMEM_SPEC] * 5, tile=small, which=None, pick=False, estimate=COST_OTHER,
            )(*arguments)
            continue
        arguments += (resident(drives),)
        if instant + 1 == SLOTS:
            return call(
                last_kernel, jax.ShapeDtypeStruct((trials, columns), F32), [VMEM_SPEC] * 6,
                [pltpu.VMEM((trials, columns), F32), copies((columns // half,))], ANY_SPEC, tile=half, which=which,
            )(*arguments)[None]
        if instant + 1 == SUB - 1:
            before = resident(rates)
            x, rates, recent = call(
                other_kernel, (wide, narrow, pltpu.VMEM((block_rows(SUB, trials, chosen), 128), BF16)), [VMEM_SPEC] * 9,
                tile=small, which=which, pick=True, estimate=COST_OTHER,
            )(*arguments, select, first_rates, before)
            recent, partial = call(
                ahead_kernel, (pltpu.VMEM(recent.shape, BF16), wide), [VMEM_SPEC] * 3, tile=tile, estimate=COST_OWN
            )(resident(recent), resident(rates), kept)
            recent = around(recent)[::-1]
            partial = call(behind_kernel, wide, [VMEM_SPEC] * 9, tile=tile, aliases={0: 0}, instant=instant + 1)(
                resident(partial), resident(rates), kept, resident(delays), stimulus, *maps, *past
            )
        else:
            x, rates = call(
                other_kernel, (wide, narrow), [VMEM_SPEC] * 6, tile=small, which=which, pick=False, estimate=COST_OTHER,
            )(*arguments)
        which += 1


def solution(mesh):
    return jax.shard_map(
        local,
        mesh=mesh,
        in_specs=(
            P("area", "row"),
            P("area", None),
            P("area", None, "groups", "row"),
            P("area", "groups", "row"),
            P("area", "groups", "row"),
            P("area", "row"),
            P("area", None, "row"),
            P("area", None, "row"),
            P("area", None, "row"),
        ),
        out_specs=P("area", "groups", "row"),
        check_vma=False,
    )
```
